128 devices in a mesh: sx: 16 (over z, x), sy: 8 (over y, core).
Axes of the slice: x: 4, y: 4, z: 4, core: 2. Of those that a mesh axis runs over, the one named last changes fastest.
Arguments:
- activations: bfloat16 [65536, 1024], P(('sx', 'sy')), may hold values from -6 to 6
- norm_gain: float32 [1024], replicated, may hold values from 0.5 to 8
- w_local: bfloat16 [1024, 1536], replicated, may hold values from -0.1875 to 0.1875
- w_cluster: bfloat16 [1024, 3072], replicated, may hold values from -0.1875 to 0.1875
- w_output: bfloat16 [1536, 1024], replicated, may hold values from -0.15625 to 0.15625
- assignment: int32 [65536, 8], P(('sx', 'sy')), may hold values from 0 to 31, as said below
Outputs:
- layer_out: bfloat16 [65536, 1024], P(('sx', 'sy'))
The draws below stay inside these ranges and needn't reach their ends.
Inputs may be any that keep to these rules, and one draw needn't show every extreme that they name: `assignment`: tokens d * 512 to (d + 1) * 512 - 1 form block d. In every head each cluster number is given to exactly 2048 tokens; at most 28 tokens of one block share a cluster number in one head, and in every head some block has exactly 28. Task group g of head h is the clusters g * 2 to (g + 1) * 2 - 1; at most 40 tokens of one block fall into one task group of one head, and in every head some block has exactly 40 in some group.
All inputs are finite; a program needn't handle non-finite values.
Results may differ from the reference program's by a relative error of at most 0.0035.
The reference program's roundings to bfloat16 on the way count: a program that leaves them out, or rounds other values in their place, can miss the bound.
Values may be sent and summed in bfloat16 or wider, within the bound.
No kernel may reach another device: no remote copies, remote signals or barrier semaphores. Data moves between devices by JAX's collectives and lax.ppermute only.
A program may use at most 128 MiB of HBM per device.

```python
import math
import jax
import jax.numpy as jnp
from jax import lax

D = 1024
HL = 4
HC = 8
HD = 128
WIN = 512
CSIZE = 2048
TOK_DEV = 512
SHARDS = 128
TOKENS = 65536
CLUSTERS = 32
TASK_DEV = 2


def draw_norm_gain(key, part):
    return jnp.exp(jax.random.uniform(key, (D,), jnp.float32, math.log(0.5), math.log(2.0)))


def count_table(key):
    mean_rows = CSIZE // SHARDS
    group_size = max(2, TASK_DEV)
    device_order = jax.random.permutation(jax.random.fold_in(key, 1), SHARDS)
    group_order = jax.random.permutation(jax.random.fold_in(key, 2), CLUSTERS // group_size)
    cluster_ids = jnp.arange(CLUSTERS, dtype=jnp.int32)
    first_device = jnp.where(device_order < SHARDS // 2, 1, -1)
    second_device = jnp.where(device_order % 2 == 0, 1, -1)
    first_cluster = jnp.where(cluster_ids % 2 == 0, 1, -1)
    second_cluster = jnp.where(group_order[cluster_ids // group_size] < CLUSTERS // (2 * group_size), 1, -1)
    first_sign = first_device[:, None] * first_cluster[None, :]
    second_sign = second_device[:, None] * second_cluster[None, :]
    return (mean_rows + mean_rows // 2 * first_sign + mean_rows // 4 * second_sign).astype(jnp.int32)


def head_assignment(key):
    table = count_table(key)
    bounds = jnp.cumsum(table, axis=1)
    places = jnp.arange(TOK_DEV, dtype=jnp.int32)
    ordered = jnp.sum((bounds[:, None, :] <= places[None, :, None]).astype(jnp.int32), axis=2)
    shuffles = jax.vmap(lambda sub_key: jax.random.permutation(sub_key, TOK_DEV))(jax.random.split(jax.random.fold_in(key, 3), SHARDS))
    return jnp.take_along_axis(ordered, shuffles, axis=1).reshape(TOKENS)


def draw_assignment(key, part):
    columns = [head_assignment(jax.random.fold_in(key, 10 + head_index)) for head_index in range(HC)]
    return jnp.stack(columns, axis=1).astype(jnp.int32)


def block_levels(own_key, dims, shards, smallest, top_value):
    factor_of = 1.0
    for dim, parts in shards:
        steps = jax.random.uniform(jax.random.fold_in(jax.random.fold_in(own_key, 6), dim), (parts,), jnp.float32, smallest / len(shards), top_value / len(shards))
        factor_of = factor_of * jnp.repeat(jnp.exp(steps), dims[dim] // parts).reshape((-1,) + (1,) * (len(dims) - 1 - dim))
    return factor_of


def normal_values(stream_key, extent, scale, limit, cuts=(), kind=jnp.bfloat16):
    gain = block_levels(stream_key, extent, cuts, -0.22, 0.18) if cuts else 1.0
    drawn = jax.random.normal(stream_key, extent, jnp.float32) * scale * gain
    return jnp.minimum(jnp.maximum(drawn, -limit), limit).astype(kind)


def setup_inputs(seed: int = 0) -> dict:
    streams_of = jax.random.split(jax.random.key(seed), 7)
    activations = normal_values(streams_of[0], (TOKENS, D), 1.0, 6.0, ((0, 128),))
    norm_gain = draw_norm_gain(jax.random.fold_in(streams_of[6], 71), 0)
    w_local = normal_values(streams_of[2], (D, 3 * HL * HD), D ** -0.5, 0.1875)
    w_cluster = normal_values(streams_of[3], (D, 3 * HC * HD), D ** -0.5, 0.1875)
    w_output = normal_values(streams_of[4], ((HL + HC) * HD, D), ((HL + HC) * HD) ** -0.5, 0.15625)
    assignment = draw_assignment(jax.random.fold_in(streams_of[6], 71), 0)
    return dict(activations=activations, norm_gain=norm_gain, w_local=w_local, w_cluster=w_cluster, w_output=w_output, assignment=assignment)


EPSILON = 1e-06

def rms_norm(activations, norm_gain):
    values = activations.astype(jnp.float32)
    mean_square = lax.optimization_barrier(jnp.mean(values * values, axis=-1, keepdims=True))
    return (values * lax.rsqrt(mean_square + EPSILON) * norm_gain).astype(jnp.bfloat16)

def normalize_rows(scores):
    highest = lax.optimization_barrier(jnp.max(scores, axis=-1, keepdims=True))
    raised = jnp.exp(scores - highest)
    return (raised / lax.optimization_barrier(jnp.sum(raised, axis=-1, keepdims=True))).astype(jnp.bfloat16)

def window_attention(local_qkv):
    head_width = HL * HD
    score_scale = HD ** (-0.5)
    queries = local_qkv[:, :head_width].astype(jnp.float32)
    key_value = jnp.concatenate([jnp.zeros((WIN, 2 * head_width), jnp.float32), local_qkv[:, head_width:].astype(jnp.float32)], axis=0)
    block_rows = min(512, TOK_DEV)

    def one_block(first_row):
        query_block = lax.dynamic_slice_in_dim(queries, first_row, block_rows, 0).reshape(block_rows, HL, HD)
        pair_block = lax.dynamic_slice_in_dim(key_value, first_row, block_rows + WIN, 0)
        key_block = pair_block[:, :head_width].reshape(block_rows + WIN, HL, HD)
        value_block = pair_block[:, head_width:].reshape(block_rows + WIN, HL, HD)
        scores = jnp.einsum('qhd,khd->hqk', query_block, key_block) * score_scale
        row_ids = jnp.arange(block_rows, dtype=jnp.int32)[:, None]
        col_ids = jnp.arange(block_rows + WIN, dtype=jnp.int32)[None, :]
        allowed = (col_ids > row_ids) & (col_ids <= row_ids + WIN) & (first_row + col_ids - WIN >= 0)
        scores = jnp.where(allowed[None], scores, -1e+30)
        weights = normalize_rows(scores).astype(jnp.float32)
        mixed = jnp.einsum('hqk,khd->qhd', weights, value_block)
        return mixed.astype(jnp.bfloat16).reshape(block_rows, head_width)
    starts = jnp.arange(TOKENS // block_rows, dtype=jnp.int32) * block_rows
    return lax.map(one_block, starts).reshape(TOKENS, head_width)

def cluster_block(packed):
    score_scale = HD ** (-0.5)
    queries = packed[:, :HD].astype(jnp.float32)
    key_rows = packed[:, HD:2 * HD].astype(jnp.float32)
    value_rows = packed[:, 2 * HD:].astype(jnp.float32)
    block_rows = min(512, CSIZE)

    def one_block(first_row):
        query_block = lax.dynamic_slice_in_dim(queries, first_row, block_rows, 0)
        scores = jnp.einsum('qd,kd->qk', query_block, key_rows) * score_scale
        weights = normalize_rows(scores).astype(jnp.float32)
        return jnp.einsum('qk,kd->qd', weights, value_rows).astype(jnp.bfloat16)
    starts = jnp.arange(CSIZE // block_rows, dtype=jnp.int32) * block_rows
    return lax.map(one_block, starts).reshape(CSIZE, HD)

def reference(activations, norm_gain, w_local, w_cluster, w_output, assignment):
    normed = rms_norm(activations, norm_gain)
    local_qkv = jnp.dot(normed, w_local, preferred_element_type=jnp.float32).astype(jnp.bfloat16)
    cluster_qkv = jnp.dot(normed, w_cluster, preferred_element_type=jnp.float32).astype(jnp.bfloat16)
    local_mix = window_attention(local_qkv)
    cluster_count = TOKENS // CSIZE
    pieces = []
    for head_index in range(HC):
        head_rows = cluster_qkv[:, head_index * 3 * HD:(head_index + 1) * 3 * HD]
        grouping = jnp.argsort(assignment[:, head_index], stable=True).astype(jnp.int32)
        grouped = head_rows[grouping].reshape(cluster_count, CSIZE, 3 * HD)
        mixed = lax.map(cluster_block, grouped).reshape(TOKENS, HD)
        pieces.append(jnp.zeros((TOKENS, HD), jnp.bfloat16).at[grouping].set(mixed))
    cluster_mix = jnp.concatenate(pieces, axis=1)
    combined = jnp.concatenate([local_mix, cluster_mix], axis=1)
    projected = jnp.dot(combined, w_output, preferred_element_type=jnp.float32)
    return (activations.astype(jnp.float32) + projected).astype(jnp.bfloat16)
```

```python
import functools
import math

import jax
import jax.numpy as jnp
from jax import lax
from jax.experimental import pallas as pl
from jax.experimental.pallas import tpu as pltpu
from jax.sharding import PartitionSpec as P

HL = 4
HC = 8
HD = 128
WIN = 512
CSIZE = 2048
CLUSTERS = 32
TOK = 512
D = 1024
SHARDS = 128
POOL = 40
PER_CLUSTER = 28
GROUPS = CLUSTERS // 2
REGION = GROUPS * POOL
CHUNK = 8
CHUNKS = SHARDS // CHUNK
CHUNK_ROWS = CHUNK * POOL
SPAN = CHUNK * PER_CLUSTER + 16
QBLOCK = 256
EPSILON = 1e-06
AXES = ("sx", "sy")
VMEM = 60 * 2**20
EXP2_SCALE = HD ** (-0.5) * math.log2(math.e)
NT = (((1,), (1,)), ((), ()))
TN = (((0,), (0,)), ((), ()))
F32 = jnp.float32
BF16 = jnp.bfloat16


def iota(shape, dim):
    return lax.broadcasted_iota(jnp.int32, shape, dim)


def one_hot(condition):
    return jnp.where(condition, 1.0, 0.0).astype(BF16)


def rms_norm(activations, norm_gain):
    values = activations.astype(F32)
    mean_square = jnp.mean(values * values, axis=-1, keepdims=True)
    return (values * lax.rsqrt(mean_square + EPSILON) * norm_gain).astype(BF16)


def slot_of(cluster, position):
    return (cluster >> 1) * POOL + jnp.where((cluster & 1) == 1, POOL - 1 - position, position)


def pre_kernel(act_ref, gain_ref, w_ref, asg_ref, out_ref, normed, slots):
    head = pl.program_id(0)

    @pl.when(head == 0)
    def _():
        normed[...] = rms_norm(act_ref[...], gain_ref[...])
        asg = asg_ref[...].astype(F32).astype(BF16)
        spread = one_hot((iota((HC * CLUSTERS, HC), 0) >> 5) == iota((HC * CLUSTERS, HC), 1))
        value = lax.dot_general(spread, asg, NT, preferred_element_type=F32)
        member = value == (iota((HC * CLUSTERS, TOK), 0) & (CLUSTERS - 1)).astype(F32)
        before = one_hot(iota((TOK, TOK), 0) < iota((TOK, TOK), 1))
        running = jnp.dot(one_hot(member), before, preferred_element_type=F32)
        gather = one_hot(iota((HC, HC * CLUSTERS), 0) == (iota((HC, HC * CLUSTERS), 1) >> 5))
        position = jnp.dot(
            gather, jnp.where(member, running, 0.0).astype(BF16), preferred_element_type=F32
        ).astype(jnp.int32)
        eye = one_hot(iota((HC, HC), 0) == iota((HC, HC), 1))
        cluster = lax.dot_general(eye, asg, NT, preferred_element_type=F32).astype(jnp.int32)
        slot = slot_of(cluster, position)
        for index in range(HC):
            slots[index] = slot[index : index + 1]

    qkv = jnp.dot(normed[...], w_ref[...], preferred_element_type=F32).astype(BF16)
    table = one_hot(iota((REGION, TOK), 0) == slots[head])
    out_ref[...] = jnp.dot(table, qkv, preferred_element_type=F32).astype(BF16)


def pre_call(activations, norm_gain, w_cluster, assignment):
    return pl.pallas_call(
        pre_kernel,
        grid=(HC,),
        in_specs=[
            pl.BlockSpec((TOK, D), lambda h: (0, 0)),
            pl.BlockSpec((1, D), lambda h: (0, 0)),
            pl.BlockSpec((D, 3 * HD), lambda h: (0, h)),
            pl.BlockSpec((TOK, HC), lambda h: (0, 0)),
        ],
        out_specs=pl.BlockSpec((REGION, 3 * HD), lambda h: (h, 0)),
        out_shape=jax.ShapeDtypeStruct((SHARDS * POOL, 3 * HD), BF16),
        scratch_shapes=[pltpu.VMEM((TOK, D), BF16), pltpu.VMEM((HC, 1, TOK), jnp.int32)],
        compiler_params=pltpu.CompilerParams(vmem_limit_bytes=VMEM),
        name="place",
    )(activations, norm_gain.reshape(1, D), w_cluster, assignment)


def softmax_rows(scores):
    highest = jnp.max(scores, axis=-1, keepdims=True)
    raised = jnp.exp2((scores - highest) * EXP2_SCALE)
    total = jnp.sum(raised, axis=-1, keepdims=True)
    return (raised * (1.0 / total)).astype(BF16)


def window_kernel(first_ref, qkv_ref, rim_ref, act_ref, w_ref, out_ref, mix):
    width = HL * HD
    step = 128
    shift = jnp.where(first_ref[0] == 0, WIN, 0)
    for head in range(HL):
        lanes = slice(head * HD, (head + 1) * HD)
        key_lanes = slice(width + head * HD, width + (head + 1) * HD)
        value_lanes = slice(2 * width + head * HD, 2 * width + (head + 1) * HD)
        for low in range(0, TOK, step):
            high = low + step
            query = qkv_ref[low:high, lanes]
            keys = jnp.concatenate([rim_ref[low:, lanes], qkv_ref[:high, key_lanes]], axis=0)
            values = jnp.concatenate(
                [rim_ref[low:, key_lanes], qkv_ref[:high, value_lanes]], axis=0
            )
            scores = lax.dot_general(query, keys, NT, preferred_element_type=F32)
            rows = iota(scores.shape, 0)
            cols = iota(scores.shape, 1)
            allowed = (cols > rows) & (cols <= rows + WIN) & (cols + low >= shift)
            weights = softmax_rows(jnp.where(allowed, scores, -1e30))
            mix[low:high, lanes] = jnp.dot(weights, values, preferred_element_type=F32).astype(BF16)
    out_ref[...] = act_ref[...].astype(F32) + jnp.dot(
        mix[...], w_ref[...], preferred_element_type=F32
    )


def window_call(first, local_qkv, rim, activations, w_output):
    width = HL * HD
    return pl.pallas_call(
        window_kernel,
        grid=(1,),
        in_specs=[
            pl.BlockSpec(memory_space=pltpu.SMEM),
            pl.BlockSpec((TOK, 3 * width), lambda i: (0, 0)),
            pl.BlockSpec((WIN, 2 * width), lambda i: (0, 0)),
            pl.BlockSpec((TOK, D), lambda i: (0, 0)),
            pl.BlockSpec((width, D), lambda i: (0, 0)),
        ],
        out_specs=pl.BlockSpec((TOK, D), lambda i: (0, 0)),
        out_shape=jax.ShapeDtypeStruct((TOK, D), F32),
        scratch_shapes=[pltpu.VMEM((TOK, width), BF16)],
        compiler_params=pltpu.CompilerParams(vmem_limit_bytes=VMEM),
        cost_estimate=pl.CostEstimate(flops=10**10, bytes_accessed=10**7, transcendentals=0),
        name="window",
    )(first, local_qkv, rim, activations, w_output)


def cluster_kernel(base_ref, pool_ref, rel_ref, out_ref, packed, mixed):
    packed[:, :16] = jnp.zeros((2, 16, 3 * HD), BF16)
    mixed[:, CSIZE:] = jnp.zeros((2, SPAN, HD), BF16)

    @pl.loop(0, CHUNKS)
    def _(chunk):
        rows = pool_ref[pl.ds(pl.multiple_of(chunk * CHUNK_ROWS, 16), CHUNK_ROWS), :]
        for which in range(2):
            index = chunk * 2 + which
            base = pl.multiple_of(base_ref[index], 16)
            table = one_hot(iota((SPAN, CHUNK_ROWS), 0) == rel_ref[index])
            moved = jnp.dot(table, rows, preferred_element_type=F32).astype(BF16)
            packed[which, pl.ds(base, 16), :] += moved[:16]
            packed[which, pl.ds(pl.multiple_of(base + 16, 16), SPAN - 16), :] = moved[16:]

    for which in range(2):

        @pl.loop(0, CSIZE // QBLOCK)
        def _(block):
            place = pl.ds(pl.multiple_of(block * QBLOCK, QBLOCK), QBLOCK)
            query = packed[which, place, :HD]
            scores = lax.dot_general(
                query, packed[which, :CSIZE, HD : 2 * HD], NT, preferred_element_type=F32
            )
            weights = softmax_rows(scores)
            mixed[which, place, :] = jnp.dot(
                weights, packed[which, :CSIZE, 2 * HD :], preferred_element_type=F32
            ).astype(BF16)

    @pl.loop(0, CHUNKS)
    def _(chunk):
        total = jnp.zeros((CHUNK_ROWS, HD), F32)
        for which in range(2):
            index = chunk * 2 + which
            base = pl.multiple_of(base_ref[index], 16)
            table = one_hot(iota((SPAN, CHUNK_ROWS), 0) == rel_ref[index])
            total += lax.dot_general(
                table, mixed[which, pl.ds(base, SPAN), :], TN, preferred_element_type=F32
            )
        out_ref[pl.ds(pl.multiple_of(chunk * CHUNK_ROWS, 16), CHUNK_ROWS), :] = total.astype(BF16)


def cluster_call(bases, pool, rel):
    return pl.pallas_call(
        cluster_kernel,
        in_specs=[
            pl.BlockSpec(memory_space=pltpu.SMEM),
            pl.BlockSpec(memory_space=pltpu.VMEM),
            pl.BlockSpec(memory_space=pltpu.VMEM),
        ],
        out_specs=pl.BlockSpec(memory_space=pltpu.VMEM),
        out_shape=jax.ShapeDtypeStruct((SHARDS * POOL, HD), BF16),
        scratch_shapes=[
            pltpu.VMEM((2, CSIZE + SPAN, 3 * HD), BF16),
            pltpu.VMEM((2, CSIZE + SPAN, HD), BF16),
        ],
        compiler_params=pltpu.CompilerParams(vmem_limit_bytes=VMEM),
        name="cluster",
    )(bases, pool, rel)


def post_kernel(back_ref, slot_ref, base_ref, w_ref, out_ref, total):
    step = pl.program_id(0)

    @pl.when(step == 0)
    def _():
        total[...] = base_ref[...]

    parts = []
    for inner in range(2):
        pick = iota((TOK, HC), 1) == step * 2 + inner
        slot = jnp.sum(jnp.where(pick, slot_ref[...], 0), axis=1, keepdims=True)
        table = one_hot(iota((TOK, REGION), 1) == slot)
        rows = back_ref[inner * REGION : (inner + 1) * REGION, :]
        parts.append(jnp.dot(table, rows, preferred_element_type=F32).astype(BF16))
    mix = jnp.concatenate(parts, axis=1)
    total[...] += jnp.dot(mix, w_ref[...], preferred_element_type=F32)

    @pl.when(step == HC // 2 - 1)
    def _():
        out_ref[...] = total[...].astype(BF16)


def post_call(back, slot, base, w_output):
    return pl.pallas_call(
        post_kernel,
        grid=(HC // 2,),
        in_specs=[
            pl.BlockSpec((2 * REGION, HD), lambda h: (h, 0)),
            pl.BlockSpec((TOK, HC), lambda h: (0, 0)),
            pl.BlockSpec((TOK, D), lambda h: (0, 0)),
            pl.BlockSpec((2 * HD, D), lambda h: (h + HL // 2, 0)),
        ],
        out_specs=pl.BlockSpec((TOK, D), lambda h: (0, 0)),
        out_shape=jax.ShapeDtypeStruct((TOK, D), BF16),
        scratch_shapes=[pltpu.VMEM((TOK, D), F32)],
        compiler_params=pltpu.CompilerParams(vmem_limit_bytes=VMEM),
        name="collect",
    )(back, slot, base, w_output)


def token_slots(assignment):
    member = assignment[:, :, None] == jnp.arange(CLUSTERS, dtype=jnp.int32)
    rows = jnp.arange(TOK, dtype=jnp.int32)
    earlier = (rows[:, None] > rows[None, :]).astype(BF16)
    running = jnp.dot(
        earlier, member.astype(BF16).reshape(TOK, HC * CLUSTERS), preferred_element_type=F32
    ).reshape(TOK, HC, CLUSTERS)
    position = jnp.sum(jnp.where(member, running, 0.0), axis=2).astype(jnp.int32)
    return slot_of(assignment, position)


def compaction_plan(counts):
    sources = jnp.arange(SHARDS, dtype=jnp.int32)
    earlier = (sources[:, None] > sources[None, :]).astype(BF16)
    start = jnp.dot(earlier, counts.astype(BF16), preferred_element_type=F32).astype(jnp.int32)
    bases = start.reshape(CHUNKS, CHUNK, 2)[:, 0, :] // 16 * 16
    local = (start.reshape(CHUNKS, CHUNK, 2) - bases[:, None, :]).reshape(SHARDS, 2)
    places = jnp.arange(POOL, dtype=jnp.int32)
    order = jnp.stack([places, POOL - 1 - places])
    inside = order[None] < counts[:, :, None]
    rel = jnp.where(inside, local[:, :, None] + order[None], -1)
    rel = rel.reshape(CHUNKS, CHUNK, 2, POOL).transpose(0, 2, 1, 3)
    return bases.reshape(2 * CHUNKS), rel.reshape(2 * CHUNKS, 1, CHUNK_ROWS)


def body(activations, norm_gain, w_local, w_cluster, w_output, assignment):
    device = lax.axis_index(AXES)
    member = assignment[:, :, None] == jnp.arange(CLUSTERS, dtype=jnp.int32)
    counts = jnp.sum(member.astype(jnp.int32), axis=0).reshape(SHARDS, 2)
    got_counts = lax.all_to_all(counts, AXES, split_axis=0, concat_axis=0, tiled=True)

    placed = pre_call(activations, norm_gain, w_cluster, assignment)
    placed, got_counts = lax.optimization_barrier((placed, got_counts))
    got_pool = lax.all_to_all(
        placed.reshape(SHARDS, POOL, 3 * HD), AXES, split_axis=0, concat_axis=0, tiled=True
    )

    local_qkv = jnp.dot(
        rms_norm(activations, norm_gain), w_local, preferred_element_type=F32
    ).astype(BF16)
    slot = token_slots(assignment)
    bases, rel = compaction_plan(got_counts)

    got_pool, local_kv, bases, rel, slot = lax.optimization_barrier(
        (got_pool, local_qkv[:, HL * HD :], bases, rel, slot)
    )
    rim = lax.ppermute(local_kv, AXES, [(i, i + 1) for i in range(SHARDS - 1)])
    finished = cluster_call(bases, got_pool.reshape(SHARDS * POOL, 3 * HD), rel)
    finished, rim = lax.optimization_barrier((finished, rim))
    came_back = lax.all_to_all(
        finished.reshape(SHARDS, POOL, HD), AXES, split_axis=0, concat_axis=0, tiled=True
    )
    base = window_call(
        jnp.minimum(device, 1).astype(jnp.int32).reshape(1), local_qkv, rim, activations, w_output
    )
    return post_call(came_back.reshape(SHARDS * POOL, HD), slot, base, w_output)


def solution(mesh):
    in_specs = (P(AXES, None), P(), P(), P(), P(), P(AXES, None))
    out_specs = P(AXES, None)
    return jax.shard_map(body, mesh=mesh, in_specs=in_specs, out_specs=out_specs, check_vma=False)
```

```python
import functools
import math

import jax
import jax.numpy as jnp
from jax import lax
from jax.experimental import pallas as pl
from jax.experimental.pallas import tpu as pltpu
from jax.sharding import PartitionSpec as P

HL = 4
HC = 8
HD = 128
WIN = 512
CSIZE = 2048
CLUSTERS = 32
TOK = 512
D = 1024
SHARDS = 128
POOL = 40
PER_CLUSTER = 28
GROUPS = CLUSTERS // 2
REGION = GROUPS * POOL
MAIN = 32
TAIL = POOL - MAIN
PACK = 3 * MAIN + 4 * TAIL
HEADS_STEP = 2
CHUNK = 4
CHUNKS = SHARDS // CHUNK
CHUNK_ROWS = CHUNK * POOL
SPAN = CHUNK * PER_CLUSTER + 16
QBLOCK = 512
EPSILON = 1e-06
AXES = ("sx", "sy")
VMEM = 60 * 2**20
EXP2_SCALE = HD ** (-0.5) * math.log2(math.e)
NT = (((1,), (1,)), ((), ()))
TN = (((0,), (0,)), ((), ()))
F32 = jnp.float32
BF16 = jnp.bfloat16


def iota(shape, dim):
    return lax.broadcasted_iota(jnp.int32, shape, dim)


def one_hot(condition):
    return jnp.where(condition, 1.0, 0.0).astype(BF16)


def rms_norm(activations, norm_gain):
    values = activations.astype(F32)
    mean_square = jnp.mean(values * values, axis=-1, keepdims=True)
    return (values * lax.rsqrt(mean_square + EPSILON) * norm_gain).astype(BF16)


def slot_of(cluster, position):
    return jnp.where((cluster & 1) == 1, POOL - 1 - position, position)


def pre_kernel(act_ref, gain_ref, w_ref, asg_ref, out_ref, normed, rows, sizes):
    step = pl.program_id(0)

    @pl.when(step == 0)
    def _():
        normed[...] = rms_norm(act_ref[...], gain_ref[...])
        cluster = asg_ref[...]
        spread = one_hot((iota((HC * CLUSTERS, HC), 0) >> 5) == iota((HC * CLUSTERS, HC), 1))
        value = jnp.dot(spread, cluster.astype(F32).astype(BF16), preferred_element_type=F32)
        member = value == (iota((HC * CLUSTERS, TOK), 0) & (CLUSTERS - 1)).astype(F32)
        before = one_hot(iota((TOK, TOK), 0) < iota((TOK, TOK), 1))
        running = jnp.dot(one_hot(member), before, preferred_element_type=F32)
        gather = one_hot(iota((HC, HC * CLUSTERS), 0) == (iota((HC, HC * CLUSTERS), 1) >> 5))
        position = jnp.dot(
            gather, jnp.where(member, running, 0.0).astype(BF16), preferred_element_type=F32
        ).astype(jnp.int32)
        slot = slot_of(cluster, position)
        group = cluster >> 1
        row = jnp.where(
            slot < MAIN, group * MAIN + slot, GROUPS * MAIN + group * TAIL + slot - MAIN
        )
        for index in range(HC):
            rows[index] = row[index : index + 1]
        sizes[...] = jnp.dot(
            one_hot(member), jnp.ones((TOK, HD), BF16), preferred_element_type=F32
        ).astype(BF16)

    qkv = jnp.dot(normed[...], w_ref[...], preferred_element_type=F32).astype(BF16)
    which = iota((GROUPS * TAIL, CLUSTERS), 0)
    pick = one_hot(
        ((which >> 3) * 2 + (which & 7) == iota((GROUPS * TAIL, CLUSTERS), 1)) & ((which & 7) < 2)
    )
    for inner in range(HEADS_STEP):
        head = step * HEADS_STEP + inner
        table = one_hot(iota((REGION, TOK), 0) == rows[head])
        placed = jnp.dot(
            table, qkv[:, inner * 3 * HD : (inner + 1) * 3 * HD], preferred_element_type=F32
        )
        size = sizes[pl.ds(pl.multiple_of(head * CLUSTERS, CLUSTERS), CLUSTERS), :]
        tails = []
        groups = slice(inner * GROUPS, (inner + 1) * GROUPS)
        for kind in range(3):
            part = placed[:, kind * HD : (kind + 1) * HD]
            out_ref[groups, kind * MAIN : (kind + 1) * MAIN, :] = (
                part[: GROUPS * MAIN].astype(BF16).reshape(GROUPS, MAIN, HD)
            )
            tails.append(part[GROUPS * MAIN :].reshape(GROUPS, TAIL, HD))
        tails.append(jnp.dot(pick, size, preferred_element_type=F32).reshape(GROUPS, TAIL, HD))
        out_ref[groups, 3 * MAIN :, :] = jnp.concatenate(tails, axis=1).astype(BF16)


def pre_call(activations, norm_gain, w_cluster, assignment):
    return pl.pallas_call(
        pre_kernel,
        grid=(HC // HEADS_STEP,),
        in_specs=[
            pl.BlockSpec((TOK, D), lambda h: (0, 0)),
            pl.BlockSpec((1, D), lambda h: (0, 0)),
            pl.BlockSpec((D, HEADS_STEP * 3 * HD), lambda h: (0, h)),
            pl.BlockSpec((HC, TOK), lambda h: (0, 0)),
        ],
        out_specs=pl.BlockSpec((HEADS_STEP * GROUPS, PACK, HD), lambda h: (h, 0, 0)),
        out_shape=jax.ShapeDtypeStruct((SHARDS, PACK, HD), BF16),
        scratch_shapes=[
            pltpu.VMEM((TOK, D), BF16),
            pltpu.VMEM((HC, 1, TOK), jnp.int32),
            pltpu.VMEM((HC * CLUSTERS, HD), BF16),
        ],
        compiler_params=pltpu.CompilerParams(vmem_limit_bytes=VMEM),
        name="place",
    )(activations, norm_gain.reshape(1, D), w_cluster, assignment.T)


def softmax_of(scores, axis):
    highest = jnp.max(scores, axis=axis, keepdims=True)
    raised = jnp.exp2((scores - highest) * EXP2_SCALE)
    total = jnp.sum(raised, axis=axis, keepdims=True)
    return (raised * (1.0 / total)).astype(BF16)


def window_kernel(first_ref, qkv_ref, rim_ref, act_ref, w_ref, out_ref, mix):
    width = HL * HD
    step = 128
    shift = jnp.where(first_ref[0] == 0, WIN, 0)
    for head in range(HL):
        lanes = slice(head * HD, (head + 1) * HD)
        key_lanes = slice(width + head * HD, width + (head + 1) * HD)
        value_lanes = slice(2 * width + head * HD, 2 * width + (head + 1) * HD)
        for low in range(0, TOK, step):
            high = low + step
            query = qkv_ref[low:high, lanes]
            keys = jnp.concatenate([rim_ref[low:, lanes], qkv_ref[:high, key_lanes]], axis=0)
            values = jnp.concatenate(
                [rim_ref[low:, key_lanes], qkv_ref[:high, value_lanes]], axis=0
            )
            scores = lax.dot_general(query, keys, NT, preferred_element_type=F32)
            rows = iota(scores.shape, 0)
            cols = iota(scores.shape, 1)
            allowed = (cols > rows) & (cols <= rows + WIN) & (cols + low >= shift)
            weights = softmax_of(jnp.where(allowed, scores, -1e30), 1)
            mix[low:high, lanes] = jnp.dot(weights, values, preferred_element_type=F32).astype(BF16)
    out_ref[...] = act_ref[...].astype(F32) + jnp.dot(
        mix[...], w_ref[...], preferred_element_type=F32
    )


def window_call(first, local_qkv, rim, activations, w_output):
    width = HL * HD
    return pl.pallas_call(
        window_kernel,
        grid=(1,),
        in_specs=[
            pl.BlockSpec(memory_space=pltpu.SMEM),
            pl.BlockSpec((TOK, 3 * width), lambda i: (0, 0)),
            pl.BlockSpec((WIN, 2 * width), lambda i: (0, 0)),
            pl.BlockSpec((TOK, D), lambda i: (0, 0)),
            pl.BlockSpec((width, D), lambda i: (0, 0)),
        ],
        out_specs=pl.BlockSpec((TOK, D), lambda i: (0, 0)),
        out_shape=jax.ShapeDtypeStruct((TOK, D), F32),
        scratch_shapes=[pltpu.VMEM((TOK, width), BF16)],
        compiler_params=pltpu.CompilerParams(vmem_limit_bytes=VMEM),
        cost_estimate=pl.CostEstimate(flops=10**10, bytes_accessed=10**7, transcendentals=0),
        name="window",
    )(first, local_qkv, rim, activations, w_output)


def plan_moves(pool_ref, main_rows, tail_rows, first_rows):
    source = iota((SHARDS, SHARDS), 0)
    other = iota((SHARDS, SHARDS), 1)
    earlier = one_hot(other < source)
    chunk_earlier = one_hot(other < (source & ~(CHUNK - 1)))
    own_lanes = (source & (CHUNK - 1)) == (other >> 5)
    chunk_of = one_hot(iota((CHUNKS, SHARDS), 0) == (iota((CHUNKS, SHARDS), 1) >> 2))
    leader = one_hot(iota((CHUNKS, SHARDS), 0) * CHUNK == iota((CHUNKS, SHARDS), 1))
    place = iota((CHUNKS, SHARDS), 1) & (MAIN - 1)
    tail_block = pool_ref[:, PACK - 16 :, :].reshape(SHARDS * 16, HD)
    picked = iota((SHARDS, SHARDS * 16), 1) - iota((SHARDS, SHARDS * 16), 0) * 16
    starts, sizes, firsts = [], [], []
    for which in range(2):
        size = jnp.dot(
            one_hot(picked == 8 + which), tail_block, preferred_element_type=F32
        ).astype(BF16)
        start = jnp.dot(earlier, size, preferred_element_type=F32).astype(jnp.int32)
        first = jnp.dot(chunk_earlier, size, preferred_element_type=F32).astype(jnp.int32) >> 4
        local = (start - (first << 4)).astype(F32)
        starts.append(
            jnp.dot(
                chunk_of,
                jnp.where(own_lanes, local, 0.0).astype(BF16),
                preferred_element_type=F32,
            ).astype(jnp.int32)
        )
        sizes.append(
            jnp.dot(
                chunk_of,
                jnp.where(own_lanes, size.astype(F32), 0.0).astype(BF16),
                preferred_element_type=F32,
            ).astype(jnp.int32)
        )
        firsts.append(
            jnp.dot(leader, first.astype(F32).astype(BF16), preferred_element_type=F32).astype(
                jnp.int32
            )
            << 4
        )

    def moves(slot, real):
        last = POOL - 1 - slot
        target = jnp.where(
            slot < sizes[0],
            starts[0] + slot,
            jnp.where(last < sizes[1], SPAN + starts[1] + last, -1),
        )
        return jnp.where(real, target, -1)

    main_rows[...] = moves(place, place >= 0)
    for kind in range(3):
        inside = (place >= kind * TAIL) & (place < (kind + 1) * TAIL)
        tail_rows[kind] = moves(place - kind * TAIL + MAIN, inside)
    first_rows[...] = jnp.where(iota((CHUNKS, SHARDS), 1) == 0, firsts[0], firsts[1])


def cluster_kernel(
    pool_ref, out_ref, packed, mixed, scores, turned, main_rows, tail_rows, first_rows, firsts, sem
):
    plan_moves(pool_ref, main_rows, tail_rows, first_rows)
    copy = pltpu.make_async_copy(first_rows, firsts, sem)
    copy.start()
    packed[:, :, :16] = jnp.zeros((3, 2, 16, HD), BF16)
    mixed[:, CSIZE:] = jnp.zeros((2, SPAN, HD), BF16)
    copy.wait()
    row_ids = iota((2 * SPAN, SHARDS), 0)

    @pl.loop(0, CHUNKS, unroll=2)
    def _(chunk):
        here = pl.ds(chunk, 1)
        sources = pl.ds(chunk * CHUNK, CHUNK)
        main_table = one_hot(row_ids == main_rows[here, :])
        tail = pool_ref[sources, 3 * MAIN :, :].reshape(CHUNK * MAIN, HD)
        for kind in range(3):
            main = pool_ref[sources, kind * MAIN : (kind + 1) * MAIN, :].reshape(CHUNK * MAIN, HD)
            table = jnp.concatenate(
                [main_table, one_hot(row_ids == tail_rows[kind, here, :])], axis=1
            )
            moved = jnp.dot(
                table, jnp.concatenate([main, tail], axis=0), preferred_element_type=F32
            ).astype(BF16)
            for which in range(2):
                first = pl.multiple_of(firsts[chunk, which], 16)
                part = moved[which * SPAN : (which + 1) * SPAN]
                packed[kind, which, pl.ds(first, 16), :] += part[:16]
                packed[kind, which, pl.ds(pl.multiple_of(first + 16, 16), SPAN - 16), :] = part[16:]

    for which in range(2):
        for low in range(0, CSIZE, 256):
            turned[which, :, low : low + 256] = packed[2, which, low : low + 256, :].T

    blocks = CSIZE // QBLOCK

    def score(index):
        which = index // blocks
        place = pl.ds(pl.multiple_of(index % blocks * QBLOCK, QBLOCK), QBLOCK)
        return lax.dot_general(
            packed[1, which, :CSIZE, :],
            packed[0, which, place, :],
            NT,
            preferred_element_type=F32,
        )

    scores[0] = score(0)

    @pl.loop(0, 2 * blocks, step=2)
    def _(pair):
        for inner in range(2):
            index = pair + inner
            which = index // blocks
            place = pl.ds(pl.multiple_of(index % blocks * QBLOCK, QBLOCK), QBLOCK)
            scores[1 - inner] = score(jnp.minimum(index + 1, 2 * blocks - 1))
            weights = softmax_of(scores[inner], 0)
            mix = jnp.dot(turned[which], weights, preferred_element_type=F32)
            mixed[which, place, :] = mix.T.astype(BF16)

    @pl.loop(0, CHUNKS, unroll=2)
    def _(chunk):
        here = pl.ds(chunk, 1)
        table = jnp.concatenate(
            [one_hot(row_ids == main_rows[here, :]), one_hot(row_ids == tail_rows[0, here, :])],
            axis=1,
        )
        rows = jnp.concatenate(
            [
                mixed[which, pl.ds(pl.multiple_of(firsts[chunk, which], 16), SPAN), :]
                for which in range(2)
            ],
            axis=0,
        )
        spread = lax.dot_general(table, rows, TN, preferred_element_type=F32)
        main = spread[: CHUNK * MAIN].reshape(CHUNK, MAIN, HD)
        tail = spread[CHUNK * MAIN :].reshape(CHUNK, MAIN, HD)[:, :TAIL]
        out_ref[pl.ds(pl.multiple_of(chunk * CHUNK_ROWS, 16), CHUNK_ROWS), :] = (
            jnp.concatenate([main, tail], axis=1).reshape(CHUNK_ROWS, HD).astype(BF16)
        )


def cluster_call(pool):
    return pl.pallas_call(
        cluster_kernel,
        in_specs=[pl.BlockSpec(memory_space=pltpu.VMEM)],
        out_specs=pl.BlockSpec(memory_space=pltpu.VMEM),
        out_shape=jax.ShapeDtypeStruct((SHARDS * POOL, HD), BF16),
        scratch_shapes=[
            pltpu.VMEM((3, 2, CSIZE + SPAN, HD), BF16),
            pltpu.VMEM((2, CSIZE + SPAN, HD), BF16),
            pltpu.VMEM((2, CSIZE, QBLOCK), F32),
            pltpu.VMEM((2, HD, CSIZE), BF16),
            pltpu.VMEM((CHUNKS, SHARDS), jnp.int32),
            pltpu.VMEM((3, CHUNKS, SHARDS), jnp.int32),
            pltpu.VMEM((CHUNKS, SHARDS), jnp.int32),
            pltpu.SMEM((CHUNKS, SHARDS), jnp.int32),
            pltpu.SemaphoreType.DMA,
        ],
        compiler_params=pltpu.CompilerParams(vmem_limit_bytes=VMEM),
        name="cluster",
    )(pool)


def post_kernel(back_ref, slot_ref, base_ref, w_ref, out_ref, total):
    step = pl.program_id(0)

    @pl.when(step == 0)
    def _():
        total[...] = base_ref[...]

    parts = []
    for inner in range(2):
        pick = iota((TOK, HC), 1) == step * 2 + inner
        slot = jnp.sum(jnp.where(pick, slot_ref[...], 0), axis=1, keepdims=True)
        table = one_hot(iota((TOK, REGION), 1) == slot)
        rows = back_ref[inner * REGION : (inner + 1) * REGION, :]
        parts.append(jnp.dot(table, rows, preferred_element_type=F32).astype(BF16))
    mix = jnp.concatenate(parts, axis=1)
    total[...] += jnp.dot(mix, w_ref[...], preferred_element_type=F32)

    @pl.when(step == HC // 2 - 1)
    def _():
        out_ref[...] = total[...].astype(BF16)


def post_call(back, slot, base, w_output):
    return pl.pallas_call(
        post_kernel,
        grid=(HC // 2,),
        in_specs=[
            pl.BlockSpec((2 * REGION, HD), lambda h: (h, 0)),
            pl.BlockSpec((TOK, HC), lambda h: (0, 0)),
            pl.BlockSpec((TOK, D), lambda h: (0, 0)),
            pl.BlockSpec((2 * HD, D), lambda h: (h + HL // 2, 0)),
        ],
        out_specs=pl.BlockSpec((TOK, D), lambda h: (0, 0)),
        out_shape=jax.ShapeDtypeStruct((TOK, D), BF16),
        scratch_shapes=[pltpu.VMEM((TOK, D), F32)],
        compiler_params=pltpu.CompilerParams(vmem_limit_bytes=VMEM),
        name="collect",
    )(back, slot, base, w_output)


def token_slots(assignment):
    member = assignment[:, :, None] == jnp.arange(CLUSTERS, dtype=jnp.int32)
    rows = jnp.arange(TOK, dtype=jnp.int32)
    earlier = (rows[:, None] > rows[None, :]).astype(BF16)
    running = jnp.dot(
        earlier, member.astype(BF16).reshape(TOK, HC * CLUSTERS), preferred_element_type=F32
    ).reshape(TOK, HC, CLUSTERS)
    position = jnp.sum(jnp.where(member, running, 0.0), axis=2).astype(jnp.int32)
    return (assignment >> 1) * POOL + slot_of(assignment, position)


def body(activations, norm_gain, w_local, w_cluster, w_output, assignment):
    device = lax.axis_index(AXES)
    placed = pre_call(activations, norm_gain, w_cluster, assignment)
    got_pool = lax.all_to_all(placed, AXES, split_axis=0, concat_axis=0, tiled=True)

    local_qkv = jnp.dot(
        rms_norm(activations, norm_gain), w_local, preferred_element_type=F32
    ).astype(BF16)
    slot = token_slots(assignment)

    got_pool, local_kv, slot = lax.optimization_barrier(
        (got_pool, local_qkv[:, HL * HD :], slot)
    )
    rim = lax.ppermute(local_kv, AXES, [(i, i + 1) for i in range(SHARDS - 1)])
    finished = cluster_call(got_pool)
    finished, rim = lax.optimization_barrier((finished, rim))
    came_back = lax.all_to_all(
        finished.reshape(SHARDS, POOL, HD), AXES, split_axis=0, concat_axis=0, tiled=True
    )
    base = window_call(
        jnp.minimum(device, 1).astype(jnp.int32).reshape(1), local_qkv, rim, activations, w_output
    )
    return post_call(came_back.reshape(SHARDS * POOL, HD), slot, base, w_output)


def solution(mesh):
    in_specs = (P(AXES, None), P(), P(), P(), P(), P(AXES, None))
    out_specs = P(AXES, None)
    return jax.shard_map(body, mesh=mesh, in_specs=in_specs, out_specs=out_specs, check_vma=False)
```

```python
import functools
import math

import jax
import jax.numpy as jnp
from jax import lax
from jax.experimental import pallas as pl
from jax.experimental.pallas import tpu as pltpu
from jax.sharding import PartitionSpec as P

HL = 4
HC = 8
HD = 128
WIN = 512
CSIZE = 2048
CLUSTERS = 32
TOK = 512
D = 1024
SHARDS = 128
POOL = 40
PER_CLUSTER = 28
GROUPS = CLUSTERS // 2
REGION = GROUPS * POOL
MAIN = 32
TAIL = POOL - MAIN
PACK = 3 * MAIN + 4 * TAIL
HEADS_STEP = 2
CHUNK = 4
CHUNKS = SHARDS // CHUNK
CHUNK_ROWS = CHUNK * POOL
SPAN = CHUNK * PER_CLUSTER + 16
QBLOCK = 512
PARTS = 4
EPSILON = 1e-06
AXES = ("sx", "sy")
VMEM = 60 * 2**20
EXP2_SCALE = HD ** (-0.5) * math.log2(math.e)
NT = (((1,), (1,)), ((), ()))
TN = (((0,), (0,)), ((), ()))
F32 = jnp.float32
BF16 = jnp.bfloat16


def iota(shape, dim):
    return lax.broadcasted_iota(jnp.int32, shape, dim)


def one_hot(condition):
    return jnp.where(condition, 1.0, 0.0).astype(BF16)


def rms_norm(activations, norm_gain):
    values = activations.astype(F32)
    mean_square = jnp.mean(values * values, axis=-1, keepdims=True)
    return (values * lax.rsqrt(mean_square + EPSILON) * norm_gain).astype(BF16)


def slot_of(cluster, position):
    return jnp.where((cluster & 1) == 1, POOL - 1 - position, position)


def pre_kernel(act_ref, gain_ref, w_ref, asg_ref, out_ref, normed, rows, sizes):
    step = pl.program_id(0)

    @pl.when(step == 0)
    def _():
        normed[...] = rms_norm(act_ref[...], gain_ref[...])
        cluster = asg_ref[...]
        spread = one_hot((iota((HC * CLUSTERS, HC), 0) >> 5) == iota((HC * CLUSTERS, HC), 1))
        value = jnp.dot(spread, cluster.astype(F32).astype(BF16), preferred_element_type=F32)
        member = value == (iota((HC * CLUSTERS, TOK), 0) & (CLUSTERS - 1)).astype(F32)
        before = one_hot(iota((TOK, TOK), 0) < iota((TOK, TOK), 1))
        running = jnp.dot(one_hot(member), before, preferred_element_type=F32)
        gather = one_hot(iota((HC, HC * CLUSTERS), 0) == (iota((HC, HC * CLUSTERS), 1) >> 5))
        position = jnp.dot(
            gather, jnp.where(member, running, 0.0).astype(BF16), preferred_element_type=F32
        ).astype(jnp.int32)
        slot = slot_of(cluster, position)
        group = cluster >> 1
        row = jnp.where(
            slot < MAIN, group * MAIN + slot, GROUPS * MAIN + group * TAIL + slot - MAIN
        )
        for index in range(HC):
            rows[index] = row[index : index + 1]
        sizes[...] = jnp.dot(
            one_hot(member), jnp.ones((TOK, HD), BF16), preferred_element_type=F32
        ).astype(BF16)

    qkv = jnp.dot(normed[...], w_ref[...], preferred_element_type=F32).astype(BF16)
    which = iota((GROUPS * TAIL, CLUSTERS), 0)
    pick = one_hot(
        ((which >> 3) * 2 + (which & 7) == iota((GROUPS * TAIL, CLUSTERS), 1)) & ((which & 7) < 2)
    )
    for inner in range(HEADS_STEP):
        head = step * HEADS_STEP + inner
        table = one_hot(iota((REGION, TOK), 0) == rows[head])
        placed = jnp.dot(
            table, qkv[:, inner * 3 * HD : (inner + 1) * 3 * HD], preferred_element_type=F32
        )
        size = sizes[pl.ds(pl.multiple_of(head * CLUSTERS, CLUSTERS), CLUSTERS), :]
        tails = []
        groups = slice(inner * GROUPS, (inner + 1) * GROUPS)
        for kind in range(3):
            part = placed[:, kind * HD : (kind + 1) * HD]
            out_ref[groups, kind * MAIN : (kind + 1) * MAIN, :] = (
                part[: GROUPS * MAIN].astype(BF16).reshape(GROUPS, MAIN, HD)
            )
            tails.append(part[GROUPS * MAIN :].reshape(GROUPS, TAIL, HD))
        tails.append(jnp.dot(pick, size, preferred_element_type=F32).reshape(GROUPS, TAIL, HD))
        out_ref[groups, 3 * MAIN :, :] = jnp.concatenate(tails, axis=1).astype(BF16)


def pre_call(activations, norm_gain, w_cluster, assignment):
    return pl.pallas_call(
        pre_kernel,
        grid=(HC // HEADS_STEP,),
        in_specs=[
            pl.BlockSpec((TOK, D), lambda h: (0, 0)),
            pl.BlockSpec((1, D), lambda h: (0, 0)),
            pl.BlockSpec((D, HEADS_STEP * 3 * HD), lambda h: (0, h)),
            pl.BlockSpec((HC, TOK), lambda h: (0, 0)),
        ],
        out_specs=pl.BlockSpec((HEADS_STEP * GROUPS, PACK, HD), lambda h: (h, 0, 0)),
        out_shape=jax.ShapeDtypeStruct((SHARDS, PACK, HD), BF16),
        scratch_shapes=[
            pltpu.VMEM((TOK, D), BF16),
            pltpu.VMEM((HC, 1, TOK), jnp.int32),
            pltpu.VMEM((HC * CLUSTERS, HD), BF16),
        ],
        compiler_params=pltpu.CompilerParams(vmem_limit_bytes=VMEM),
        name="place",
    )(activations, norm_gain.reshape(1, D), w_cluster, assignment.T)


def softmax_of(scores, axis):
    highest = jnp.max(scores, axis=axis, keepdims=True)
    raised = jnp.exp2((scores - highest) * EXP2_SCALE)
    total = jnp.sum(raised, axis=axis, keepdims=True)
    return (raised * (1.0 / total)).astype(BF16)


def window_kernel(first_ref, qkv_ref, rim_ref, act_ref, w_ref, out_ref, mix):
    width = HL * HD
    step = 128
    shift = jnp.where(first_ref[0] == 0, WIN, 0)
    for head in range(HL):
        lanes = slice(head * HD, (head + 1) * HD)
        key_lanes = slice(width + head * HD, width + (head + 1) * HD)
        value_lanes = slice(2 * width + head * HD, 2 * width + (head + 1) * HD)
        for low in range(0, TOK, step):
            high = low + step
            query = qkv_ref[low:high, lanes]
            keys = jnp.concatenate([rim_ref[low:, lanes], qkv_ref[:high, key_lanes]], axis=0)
            values = jnp.concatenate(
                [rim_ref[low:, key_lanes], qkv_ref[:high, value_lanes]], axis=0
            )
            scores = lax.dot_general(query, keys, NT, preferred_element_type=F32)
            rows = iota(scores.shape, 0)
            cols = iota(scores.shape, 1)
            allowed = (cols > rows) & (cols <= rows + WIN) & (cols + low >= shift)
            weights = softmax_of(jnp.where(allowed, scores, -1e30), 1)
            mix[low:high, lanes] = jnp.dot(weights, values, preferred_element_type=F32).astype(BF16)
    out_ref[...] = act_ref[...].astype(F32) + jnp.dot(
        mix[...], w_ref[...], preferred_element_type=F32
    )


def window_call(first, local_qkv, rim, activations, w_output):
    width = HL * HD
    return pl.pallas_call(
        window_kernel,
        grid=(1,),
        in_specs=[
            pl.BlockSpec(memory_space=pltpu.SMEM),
            pl.BlockSpec((TOK, 3 * width), lambda i: (0, 0)),
            pl.BlockSpec((WIN, 2 * width), lambda i: (0, 0)),
            pl.BlockSpec((TOK, D), lambda i: (0, 0)),
            pl.BlockSpec((width, D), lambda i: (0, 0)),
        ],
        out_specs=pl.BlockSpec((TOK, D), lambda i: (0, 0)),
        out_shape=jax.ShapeDtypeStruct((TOK, D), F32),
        scratch_shapes=[pltpu.VMEM((TOK, width), BF16)],
        compiler_params=pltpu.CompilerParams(vmem_limit_bytes=VMEM),
        cost_estimate=pl.CostEstimate(flops=10**10, bytes_accessed=10**7, transcendentals=0),
        name="window",
    )(first, local_qkv, rim, activations, w_output)


def plan_moves(meta, main_rows, tail_rows, back_rows, first_rows):
    source = iota((SHARDS, SHARDS), 0)
    other = iota((SHARDS, SHARDS), 1)
    earlier = one_hot(other < source)
    chunk_earlier = one_hot(other < (source & ~(CHUNK - 1)))
    own_lanes = (source & (CHUNK - 1)) == (other >> 5)
    chunk_of = one_hot(iota((CHUNKS, SHARDS), 0) == (iota((CHUNKS, SHARDS), 1) >> 2))
    leader = one_hot(iota((CHUNKS, SHARDS), 0) * CHUNK == iota((CHUNKS, SHARDS), 1))
    place = iota((CHUNKS, SHARDS), 1) & (MAIN - 1)
    tail_block = meta[...].reshape(SHARDS * 16, HD)
    picked = iota((SHARDS, SHARDS * 16), 1) - iota((SHARDS, SHARDS * 16), 0) * 16
    starts, sizes, firsts = [], [], []
    for which in range(2):
        size = jnp.dot(
            one_hot(picked == 8 + which), tail_block, preferred_element_type=F32
        ).astype(BF16)
        start = jnp.dot(earlier, size, preferred_element_type=F32).astype(jnp.int32)
        first = jnp.dot(chunk_earlier, size, preferred_element_type=F32).astype(jnp.int32) >> 4
        local = (start - (first << 4)).astype(F32)
        starts.append(
            jnp.dot(
                chunk_of,
                jnp.where(own_lanes, local, 0.0).astype(BF16),
                preferred_element_type=F32,
            ).astype(jnp.int32)
        )
        sizes.append(
            jnp.dot(
                chunk_of,
                jnp.where(own_lanes, size.astype(F32), 0.0).astype(BF16),
                preferred_element_type=F32,
            ).astype(jnp.int32)
        )
        firsts.append(
            jnp.dot(leader, first.astype(F32).astype(BF16), preferred_element_type=F32).astype(
                jnp.int32
            )
            << 4
        )

    def moves(slot, real):
        last = POOL - 1 - slot
        target = jnp.where(
            slot < sizes[0],
            starts[0] + slot,
            jnp.where(last < sizes[1], SPAN + starts[1] + last, -1),
        )
        return jnp.where(real, target, -1)

    main = moves(place, place >= 0)
    main_rows[...] = main
    tails = []
    for kind in range(3):
        inside = (place >= kind * TAIL) & (place < (kind + 1) * TAIL)
        tails.append(moves(place - kind * TAIL + MAIN, inside))
        tail_rows[kind] = tails[kind]
    back_rows[...] = (
        jnp.concatenate(
            [
                main.astype(F32).T.reshape(CHUNK, MAIN, CHUNKS),
                tails[0].astype(F32).T.reshape(CHUNK, MAIN, CHUNKS)[:, :TAIL],
            ],
            axis=1,
        )
        .reshape(CHUNK_ROWS, CHUNKS)
        .astype(BF16)
    )
    first_rows[...] = jnp.where(iota((CHUNKS, SHARDS), 1) == 0, firsts[0], firsts[1])


def cluster_kernel(
    pool_hbm,
    out_ref,
    pool,
    meta,
    packed,
    mixed,
    scores,
    turned,
    main_rows,
    tail_rows,
    back_rows,
    first_rows,
    firsts,
    arrived,
    planned,
):
    part = SHARDS // PARTS
    head_copy = pltpu.make_async_copy(pool_hbm.at[:, PACK - 16 :, :], meta, arrived.at[PARTS])
    head_copy.start()
    copies = []
    for index in range(PARTS):
        span = pl.ds(index * part, part)
        copies.append(pltpu.make_async_copy(pool_hbm.at[span], pool.at[span], arrived.at[index]))
        copies[index].start()
    packed[:, :, :16] = jnp.zeros((3, 2, 16, HD), BF16)
    mixed[:, CSIZE:] = jnp.zeros((2, SPAN, HD), BF16)
    head_copy.wait()
    plan_moves(meta, main_rows, tail_rows, back_rows, first_rows)
    plan_copy = pltpu.make_async_copy(first_rows, firsts, planned)
    plan_copy.start()
    plan_copy.wait()
    row_ids = iota((2 * SPAN, SHARDS), 0)

    def compact(chunk):
        here = pl.ds(chunk, 1)
        sources = pl.ds(chunk * CHUNK, CHUNK)
        main_table = one_hot(row_ids == main_rows[here, :])
        tail = pool[sources, 3 * MAIN :, :].reshape(CHUNK * MAIN, HD)
        for kind in range(3):
            main = pool[sources, kind * MAIN : (kind + 1) * MAIN, :].reshape(CHUNK * MAIN, HD)
            table = jnp.concatenate(
                [main_table, one_hot(row_ids == tail_rows[kind, here, :])], axis=1
            )
            moved = jnp.dot(
                table, jnp.concatenate([main, tail], axis=0), preferred_element_type=F32
            ).astype(BF16)
            for which in range(2):
                first = pl.multiple_of(firsts[chunk, which], 16)
                rows = moved[which * SPAN : (which + 1) * SPAN]
                packed[kind, which, pl.ds(first, 16), :] += rows[:16]
                packed[kind, which, pl.ds(pl.multiple_of(first + 16, 16), SPAN - 16), :] = rows[16:]

    for index in range(PARTS):
        copies[index].wait()
        pl.loop(index * CHUNKS // PARTS, (index + 1) * CHUNKS // PARTS, unroll=8)(compact)

    for which in range(2):
        for low in range(0, CSIZE, 256):
            turned[which, :, low : low + 256] = packed[2, which, low : low + 256, :].T

    blocks = CSIZE // QBLOCK

    def score(index):
        which = index // blocks
        place = pl.ds(pl.multiple_of(index % blocks * QBLOCK, QBLOCK), QBLOCK)
        return lax.dot_general(
            packed[1, which, :CSIZE, :],
            packed[0, which, place, :],
            NT,
            preferred_element_type=F32,
        )

    scores[0] = score(0)

    @pl.loop(0, 2 * blocks, step=2)
    def _(pair):
        for inner in range(2):
            index = pair + inner
            which = index // blocks
            place = pl.ds(pl.multiple_of(index % blocks * QBLOCK, QBLOCK), QBLOCK)
            scores[1 - inner] = score(jnp.minimum(index + 1, 2 * blocks - 1))
            weights = softmax_of(scores[inner], 0)
            mix = jnp.dot(turned[which], weights, preferred_element_type=F32)
            mixed[which, place, :] = mix.T.astype(BF16)

    @pl.loop(0, CHUNKS, unroll=8)
    def _(chunk):
        spread = one_hot(iota((CHUNKS, 2 * SPAN), 0) == chunk)
        target = jnp.dot(back_rows[...], spread, preferred_element_type=F32)
        table = one_hot(target == iota((CHUNK_ROWS, 2 * SPAN), 1).astype(F32))
        rows = jnp.concatenate(
            [
                mixed[which, pl.ds(pl.multiple_of(firsts[chunk, which], 16), SPAN), :]
                for which in range(2)
            ],
            axis=0,
        )
        out_ref[pl.ds(pl.multiple_of(chunk * CHUNK_ROWS, 16), CHUNK_ROWS), :] = jnp.dot(
            table, rows, preferred_element_type=F32
        ).astype(BF16)


def cluster_call(pool):
    return pl.pallas_call(
        cluster_kernel,
        in_specs=[pl.BlockSpec(memory_space=pl.ANY)],
        out_specs=pl.BlockSpec(memory_space=pltpu.VMEM),
        out_shape=jax.ShapeDtypeStruct((SHARDS * POOL, HD), BF16),
        scratch_shapes=[
            pltpu.VMEM((SHARDS, PACK, HD), BF16),
            pltpu.VMEM((SHARDS, 16, HD), BF16),
            pltpu.VMEM((3, 2, CSIZE + SPAN, HD), BF16),
            pltpu.VMEM((2, CSIZE + SPAN, HD), BF16),
            pltpu.VMEM((2, CSIZE, QBLOCK), F32),
            pltpu.VMEM((2, HD, CSIZE), BF16),
            pltpu.VMEM((CHUNKS, SHARDS), jnp.int32),
            pltpu.VMEM((3, CHUNKS, SHARDS), jnp.int32),
            pltpu.VMEM((CHUNK_ROWS, CHUNKS), BF16),
            pltpu.VMEM((CHUNKS, SHARDS), jnp.int32),
            pltpu.SMEM((CHUNKS, SHARDS), jnp.int32),
            pltpu.SemaphoreType.DMA((PARTS + 1,)),
            pltpu.SemaphoreType.DMA,
        ],
        compiler_params=pltpu.CompilerParams(vmem_limit_bytes=VMEM),
        name="cluster",
    )(pool)


def post_kernel(back_hbm, slot_ref, base_hbm, w_hbm, out_ref, back, base, weights, mix, sems):
    copies = []
    for index in range(HC // 2):
        span = pl.ds(index * 2 * REGION, 2 * REGION)
        copies.append(pltpu.make_async_copy(back_hbm.at[span], back.at[span], sems.at[index]))
    copies.append(
        pltpu.make_async_copy(w_hbm.at[pl.ds(HL * HD, HC * HD)], weights, sems.at[HC // 2])
    )
    copies.append(pltpu.make_async_copy(base_hbm, base, sems.at[HC // 2 + 1]))
    for copy in copies:
        copy.start()
    columns = iota((TOK, REGION), 1)
    for head in range(HC):
        if head % 2 == 0:
            copies[head // 2].wait()
        table = one_hot(columns == slot_ref[:, head : head + 1])
        mix[:, head * HD : (head + 1) * HD] = jnp.dot(
            table, back[head * REGION : (head + 1) * REGION, :], preferred_element_type=F32
        ).astype(BF16)
    copies[-2].wait()
    copies[-1].wait()
    for low in range(0, TOK, 256):
        rows = slice(low, low + 256)
        out_ref[rows, :] = (
            base[rows, :] + jnp.dot(mix[rows, :], weights[...], preferred_element_type=F32)
        ).astype(BF16)


def post_call(back, slot, base, w_output):
    return pl.pallas_call(
        post_kernel,
        in_specs=[
            pl.BlockSpec(memory_space=pl.ANY),
            pl.BlockSpec(memory_space=pltpu.VMEM),
            pl.BlockSpec(memory_space=pl.ANY),
            pl.BlockSpec(memory_space=pl.ANY),
        ],
        out_specs=pl.BlockSpec(memory_space=pltpu.VMEM),
        out_shape=jax.ShapeDtypeStruct((TOK, D), BF16),
        scratch_shapes=[
            pltpu.VMEM((HC * REGION, HD), BF16),
            pltpu.VMEM((TOK, D), F32),
            pltpu.VMEM((HC * HD, D), BF16),
            pltpu.VMEM((TOK, HC * HD), BF16),
            pltpu.SemaphoreType.DMA((HC // 2 + 2,)),
        ],
        compiler_params=pltpu.CompilerParams(vmem_limit_bytes=VMEM),
        name="collect",
    )(back, slot, base, w_output)


def token_slots(assignment):
    member = assignment[:, :, None] == jnp.arange(CLUSTERS, dtype=jnp.int32)
    rows = jnp.arange(TOK, dtype=jnp.int32)
    earlier = (rows[:, None] > rows[None, :]).astype(BF16)
    running = jnp.dot(
        earlier, member.astype(BF16).reshape(TOK, HC * CLUSTERS), preferred_element_type=F32
    ).reshape(TOK, HC, CLUSTERS)
    position = jnp.sum(jnp.where(member, running, 0.0), axis=2).astype(jnp.int32)
    return (assignment >> 1) * POOL + slot_of(assignment, position)


def body(activations, norm_gain, w_local, w_cluster, w_output, assignment):
    device = lax.axis_index(AXES)
    placed = pre_call(activations, norm_gain, w_cluster, assignment)
    got_pool = lax.all_to_all(placed, AXES, split_axis=0, concat_axis=0, tiled=True)

    local_qkv = jnp.dot(
        rms_norm(activations, norm_gain), w_local, preferred_element_type=F32
    ).astype(BF16)
    slot = token_slots(assignment)

    got_pool, local_kv, slot = lax.optimization_barrier(
        (got_pool, local_qkv[:, HL * HD :], slot)
    )
    rim = lax.ppermute(local_kv, AXES, [(i, i + 1) for i in range(SHARDS - 1)])
    finished = cluster_call(got_pool)
    finished, rim = lax.optimization_barrier((finished, rim))
    came_back = lax.all_to_all(
        finished.reshape(SHARDS, POOL, HD), AXES, split_axis=0, concat_axis=0, tiled=True
    )
    base = window_call(
        jnp.minimum(device, 1).astype(jnp.int32).reshape(1), local_qkv, rim, activations, w_output
    )
    return post_call(came_back.reshape(SHARDS * POOL, HD), slot, base, w_output)


def solution(mesh):
    in_specs = (P(AXES, None), P(), P(), P(), P(), P(AXES, None))
    out_specs = P(AXES, None)
    return jax.shard_map(body, mesh=mesh, in_specs=in_specs, out_specs=out_specs, check_vma=False)
```

```python
import functools
import math

import jax
import jax.numpy as jnp
from jax import lax
from jax.experimental import pallas as pl
from jax.experimental.pallas import tpu as pltpu
from jax.sharding import PartitionSpec as P

HL = 4
HC = 8
HD = 128
WIN = 512
CSIZE = 2048
CLUSTERS = 32
TOK = 512
D = 1024
SHARDS = 128
POOL = 40
PER_CLUSTER = 28
GROUPS = CLUSTERS // 2
REGION = GROUPS * POOL
MAIN = 32
TAIL = POOL - MAIN
PACK = 3 * MAIN + 4 * TAIL
HEADS_STEP = 2
CHUNK = 4
CHUNKS = SHARDS // CHUNK
CHUNK_ROWS = CHUNK * POOL
SPAN = CHUNK * PER_CLUSTER + 16
QBLOCK = 1024
PARTS = 4
EPSILON = 1e-06
AXES = ("sx", "sy")
VMEM = 60 * 2**20
EXP2_SCALE = HD ** (-0.5) * math.log2(math.e)
NT = (((1,), (1,)), ((), ()))
TN = (((0,), (0,)), ((), ()))
F32 = jnp.float32
BF16 = jnp.bfloat16


def iota(shape, dim):
    return lax.broadcasted_iota(jnp.int32, shape, dim)


def one_hot(condition):
    return jnp.where(condition, 1.0, 0.0).astype(BF16)


def rms_norm(activations, norm_gain):
    values = activations.astype(F32)
    mean_square = jnp.mean(values * values, axis=-1, keepdims=True)
    return (values * lax.rsqrt(mean_square + EPSILON) * norm_gain).astype(BF16)


def slot_of(cluster, position):
    return jnp.where((cluster & 1) == 1, POOL - 1 - position, position)


def pre_kernel(act_ref, gain_ref, w_ref, asg_ref, out_ref, normed, rows, sizes):
    step = pl.program_id(0)

    @pl.when(step == 0)
    def _():
        normed[...] = rms_norm(act_ref[...], gain_ref[...])
        cluster = asg_ref[...]
        spread = one_hot((iota((HC * CLUSTERS, HC), 0) >> 5) == iota((HC * CLUSTERS, HC), 1))
        value = jnp.dot(spread, cluster.astype(F32).astype(BF16), preferred_element_type=F32)
        member = value == (iota((HC * CLUSTERS, TOK), 0) & (CLUSTERS - 1)).astype(F32)
        before = one_hot(iota((TOK, TOK), 0) < iota((TOK, TOK), 1))
        running = jnp.dot(one_hot(member), before, preferred_element_type=F32)
        gather = one_hot(iota((HC, HC * CLUSTERS), 0) == (iota((HC, HC * CLUSTERS), 1) >> 5))
        position = jnp.dot(
            gather, jnp.where(member, running, 0.0).astype(BF16), preferred_element_type=F32
        ).astype(jnp.int32)
        slot = slot_of(cluster, position)
        group = cluster >> 1
        row = jnp.where(
            slot < MAIN, group * MAIN + slot, GROUPS * MAIN + group * TAIL + slot - MAIN
        )
        for index in range(HC):
            rows[index] = row[index : index + 1]
        sizes[...] = jnp.dot(
            one_hot(member), jnp.ones((TOK, HD), BF16), preferred_element_type=F32
        ).astype(BF16)

    qkv = jnp.dot(normed[...], w_ref[...], preferred_element_type=F32).astype(BF16)
    which = iota((GROUPS * TAIL, CLUSTERS), 0)
    pick = one_hot(
        ((which >> 3) * 2 + (which & 7) == iota((GROUPS * TAIL, CLUSTERS), 1)) & ((which & 7) < 2)
    )
    for inner in range(HEADS_STEP):
        head = step * HEADS_STEP + inner
        table = one_hot(iota((REGION, TOK), 0) == rows[head])
        placed = jnp.dot(
            table, qkv[:, inner * 3 * HD : (inner + 1) * 3 * HD], preferred_element_type=F32
        )
        size = sizes[pl.ds(pl.multiple_of(head * CLUSTERS, CLUSTERS), CLUSTERS), :]
        tails = []
        groups = slice(inner * GROUPS, (inner + 1) * GROUPS)
        for kind in range(3):
            part = placed[:, kind * HD : (kind + 1) * HD]
            out_ref[groups, kind * MAIN : (kind + 1) * MAIN, :] = (
                part[: GROUPS * MAIN].astype(BF16).reshape(GROUPS, MAIN, HD)
            )
            tails.append(part[GROUPS * MAIN :].reshape(GROUPS, TAIL, HD))
        tails.append(jnp.dot(pick, size, preferred_element_type=F32).reshape(GROUPS, TAIL, HD))
        out_ref[groups, 3 * MAIN :, :] = jnp.concatenate(tails, axis=1).astype(BF16)


def pre_call(activations, norm_gain, w_cluster, assignment):
    return pl.pallas_call(
        pre_kernel,
        grid=(HC // HEADS_STEP,),
        in_specs=[
            pl.BlockSpec((TOK, D), lambda h: (0, 0)),
            pl.BlockSpec((1, D), lambda h: (0, 0)),
            pl.BlockSpec((D, HEADS_STEP * 3 * HD), lambda h: (0, h)),
            pl.BlockSpec((HC, TOK), lambda h: (0, 0)),
        ],
        out_specs=pl.BlockSpec((HEADS_STEP * GROUPS, PACK, HD), lambda h: (h, 0, 0)),
        out_shape=jax.ShapeDtypeStruct((SHARDS, PACK, HD), BF16),
        scratch_shapes=[
            pltpu.VMEM((TOK, D), BF16),
            pltpu.VMEM((HC, 1, TOK), jnp.int32),
            pltpu.VMEM((HC * CLUSTERS, HD), BF16),
        ],
        compiler_params=pltpu.CompilerParams(vmem_limit_bytes=VMEM),
        name="place",
    )(activations, norm_gain.reshape(1, D), w_cluster, assignment.T)


def softmax_rows(scores):
    highest = jnp.max(scores, axis=-1, keepdims=True)
    raised = jnp.exp2((scores - highest) * EXP2_SCALE)
    total = jnp.sum(raised, axis=-1, keepdims=True)
    return (raised * (1.0 / total)).astype(BF16)


def window_kernel(first_ref, qkv_ref, rim_ref, act_ref, w_ref, out_ref, mix):
    width = HL * HD
    step = 128
    shift = jnp.where(first_ref[0] == 0, WIN, 0)
    for head in range(HL):
        lanes = slice(head * HD, (head + 1) * HD)
        key_lanes = slice(width + head * HD, width + (head + 1) * HD)
        value_lanes = slice(2 * width + head * HD, 2 * width + (head + 1) * HD)
        for low in range(0, TOK, step):
            high = low + step
            query = qkv_ref[low:high, lanes]
            keys = jnp.concatenate([rim_ref[low:, lanes], qkv_ref[:high, key_lanes]], axis=0)
            values = jnp.concatenate(
                [rim_ref[low:, key_lanes], qkv_ref[:high, value_lanes]], axis=0
            )
            scores = lax.dot_general(query, keys, NT, preferred_element_type=F32)
            rows = iota(scores.shape, 0)
            cols = iota(scores.shape, 1)
            allowed = (cols > rows) & (cols <= rows + WIN) & (cols + low >= shift)
            weights = softmax_rows(jnp.where(allowed, scores, -1e30))
            mix[low:high, lanes] = jnp.dot(weights, values, preferred_element_type=F32).astype(BF16)
    out_ref[...] = act_ref[...].astype(F32) + jnp.dot(
        mix[...], w_ref[...], preferred_element_type=F32
    )


def window_call(first, local_qkv, rim, activations, w_output):
    width = HL * HD
    return pl.pallas_call(
        window_kernel,
        grid=(1,),
        in_specs=[
            pl.BlockSpec(memory_space=pltpu.SMEM),
            pl.BlockSpec((TOK, 3 * width), lambda i: (0, 0)),
            pl.BlockSpec((WIN, 2 * width), lambda i: (0, 0)),
            pl.BlockSpec((TOK, D), lambda i: (0, 0)),
            pl.BlockSpec((width, D), lambda i: (0, 0)),
        ],
        out_specs=pl.BlockSpec((TOK, D), lambda i: (0, 0)),
        out_shape=jax.ShapeDtypeStruct((TOK, D), F32),
        scratch_shapes=[pltpu.VMEM((TOK, width), BF16)],
        compiler_params=pltpu.CompilerParams(vmem_limit_bytes=VMEM),
        cost_estimate=pl.CostEstimate(flops=10**10, bytes_accessed=10**7, transcendentals=0),
        name="window",
    )(first, local_qkv, rim, activations, w_output)


def plan_moves(meta, main_rows, tail_rows, back_rows, first_rows):
    source = iota((SHARDS, SHARDS), 0)
    other = iota((SHARDS, SHARDS), 1)
    earlier = one_hot(other < source)
    chunk_earlier = one_hot(other < (source & ~(CHUNK - 1)))
    own_lanes = (source & (CHUNK - 1)) == (other >> 5)
    chunk_of = one_hot(iota((CHUNKS, SHARDS), 0) == (iota((CHUNKS, SHARDS), 1) >> 2))
    leader = one_hot(iota((CHUNKS, SHARDS), 0) * CHUNK == iota((CHUNKS, SHARDS), 1))
    place = iota((CHUNKS, SHARDS), 1) & (MAIN - 1)
    tail_block = meta[...].reshape(SHARDS * 16, HD)
    picked = iota((SHARDS, SHARDS * 16), 1) - iota((SHARDS, SHARDS * 16), 0) * 16
    starts, sizes, firsts = [], [], []
    for which in range(2):
        size = jnp.dot(
            one_hot(picked == 8 + which), tail_block, preferred_element_type=F32
        ).astype(BF16)
        start = jnp.dot(earlier, size, preferred_element_type=F32).astype(jnp.int32)
        first = jnp.dot(chunk_earlier, size, preferred_element_type=F32).astype(jnp.int32) >> 4
        local = (start - (first << 4)).astype(F32)
        starts.append(
            jnp.dot(
                chunk_of,
                jnp.where(own_lanes, local, 0.0).astype(BF16),
                preferred_element_type=F32,
            ).astype(jnp.int32)
        )
        sizes.append(
            jnp.dot(
                chunk_of,
                jnp.where(own_lanes, size.astype(F32), 0.0).astype(BF16),
                preferred_element_type=F32,
            ).astype(jnp.int32)
        )
        firsts.append(
            jnp.dot(leader, first.astype(F32).astype(BF16), preferred_element_type=F32).astype(
                jnp.int32
            )
            << 4
        )

    def moves(slot, real):
        last = POOL - 1 - slot
        target = jnp.where(
            slot < sizes[0],
            starts[0] + slot,
            jnp.where(last < sizes[1], SPAN + starts[1] + last, -1),
        )
        return jnp.where(real, target, -1)

    main = moves(place, place >= 0)
    main_rows[...] = main
    tails = []
    for kind in range(3):
        inside = (place >= kind * TAIL) & (place < (kind + 1) * TAIL)
        tails.append(moves(place - kind * TAIL + MAIN, inside))
        tail_rows[kind] = tails[kind]
    back_rows[...] = (
        jnp.concatenate(
            [
                main.astype(F32).T.reshape(CHUNK, MAIN, CHUNKS),
                tails[0].astype(F32).T.reshape(CHUNK, MAIN, CHUNKS)[:, :TAIL],
            ],
            axis=1,
        )
        .reshape(CHUNK_ROWS, CHUNKS)
        .astype(BF16)
    )
    first_rows[...] = jnp.where(iota((CHUNKS, SHARDS), 1) == 0, firsts[0], firsts[1])


def cluster_kernel(
    pool_hbm,
    out_ref,
    pool,
    meta,
    packed,
    mixed,
    scores,
    tops,
    turned,
    main_rows,
    tail_rows,
    back_rows,
    first_rows,
    firsts,
    arrived,
    planned,
):
    part = SHARDS // PARTS
    head_copy = pltpu.make_async_copy(pool_hbm.at[:, PACK - 16 :, :], meta, arrived.at[PARTS])
    head_copy.start()
    copies = []
    for index in range(PARTS):
        span = pl.ds(index * part, part)
        copies.append(pltpu.make_async_copy(pool_hbm.at[span], pool.at[span], arrived.at[index]))
        copies[index].start()
    packed[:, :, :16] = jnp.zeros((3, 2, 16, HD), BF16)
    mixed[:, CSIZE:] = jnp.zeros((2, SPAN, HD), BF16)
    head_copy.wait()
    plan_moves(meta, main_rows, tail_rows, back_rows, first_rows)
    plan_copy = pltpu.make_async_copy(first_rows, firsts, planned)
    plan_copy.start()
    plan_copy.wait()
    row_ids = iota((2 * SPAN, SHARDS), 0)

    def compact(chunk):
        here = pl.ds(chunk, 1)
        sources = pl.ds(chunk * CHUNK, CHUNK)
        main_table = one_hot(row_ids == main_rows[here, :])
        tail = pool[sources, 3 * MAIN :, :].reshape(CHUNK * MAIN, HD)
        for kind in range(3):
            main = pool[sources, kind * MAIN : (kind + 1) * MAIN, :].reshape(CHUNK * MAIN, HD)
            table = jnp.concatenate(
                [main_table, one_hot(row_ids == tail_rows[kind, here, :])], axis=1
            )
            moved = jnp.dot(
                table, jnp.concatenate([main, tail], axis=0), preferred_element_type=F32
            ).astype(BF16)
            for which in range(2):
                first = pl.multiple_of(firsts[chunk, which], 16)
                rows = moved[which * SPAN : (which + 1) * SPAN]
                packed[kind, which, pl.ds(first, 16), :] += rows[:16]
                packed[kind, which, pl.ds(pl.multiple_of(first + 16, 16), SPAN - 16), :] = rows[16:]

    for index in range(PARTS):
        copies[index].wait()
        pl.loop(index * CHUNKS // PARTS, (index + 1) * CHUNKS // PARTS, unroll=8)(compact)

    for which in range(2):
        for low in range(0, CSIZE, 256):
            turned[which, :, low : low + 256] = packed[2, which, low : low + 256, :].T

    blocks = CSIZE // QBLOCK

    def score(buffer, index):
        which = index // blocks
        place = pl.ds(pl.multiple_of(index % blocks * QBLOCK, QBLOCK), QBLOCK)
        values = lax.dot_general(
            packed[1, which, :CSIZE, :],
            packed[0, which, place, :],
            NT,
            preferred_element_type=F32,
        )
        scores[buffer] = values
        tops[buffer] = jnp.max(values, axis=0, keepdims=True)

    score(0, 0)

    @pl.loop(0, 2 * blocks, step=2)
    def _(pair):
        for inner in range(2):
            index = pair + inner
            which = index // blocks
            place = pl.ds(pl.multiple_of(index % blocks * QBLOCK, QBLOCK), QBLOCK)
            score(1 - inner, jnp.minimum(index + 1, 2 * blocks - 1))
            raised = jnp.exp2((scores[inner] - tops[inner]) * EXP2_SCALE)
            scale = 1.0 / jnp.sum(raised, axis=0, keepdims=True)
            weights = (raised * scale).astype(BF16)
            mix = jnp.dot(turned[which], weights, preferred_element_type=F32)
            mixed[which, place, :] = mix.T.astype(BF16)

    @pl.loop(0, CHUNKS, unroll=8)
    def _(chunk):
        spread = one_hot(iota((CHUNKS, 2 * SPAN), 0) == chunk)
        target = jnp.dot(back_rows[...], spread, preferred_element_type=F32)
        table = one_hot(target == iota((CHUNK_ROWS, 2 * SPAN), 1).astype(F32))
        rows = jnp.concatenate(
            [
                mixed[which, pl.ds(pl.multiple_of(firsts[chunk, which], 16), SPAN), :]
                for which in range(2)
            ],
            axis=0,
        )
        out_ref[pl.ds(pl.multiple_of(chunk * CHUNK_ROWS, 16), CHUNK_ROWS), :] = jnp.dot(
            table, rows, preferred_element_type=F32
        ).astype(BF16)


def cluster_call(pool):
    return pl.pallas_call(
        cluster_kernel,
        in_specs=[pl.BlockSpec(memory_space=pl.ANY)],
        out_specs=pl.BlockSpec(memory_space=pltpu.VMEM),
        out_shape=jax.ShapeDtypeStruct((SHARDS * POOL, HD), BF16),
        scratch_shapes=[
            pltpu.VMEM((SHARDS, PACK, HD), BF16),
            pltpu.VMEM((SHARDS, 16, HD), BF16),
            pltpu.VMEM((3, 2, CSIZE + SPAN, HD), BF16),
            pltpu.VMEM((2, CSIZE + SPAN, HD), BF16),
            pltpu.VMEM((2, CSIZE, QBLOCK), F32),
            pltpu.VMEM((2, 1, QBLOCK), F32),
            pltpu.VMEM((2, HD, CSIZE), BF16),
            pltpu.VMEM((CHUNKS, SHARDS), jnp.int32),
            pltpu.VMEM((3, CHUNKS, SHARDS), jnp.int32),
            pltpu.VMEM((CHUNK_ROWS, CHUNKS), BF16),
            pltpu.VMEM((CHUNKS, SHARDS), jnp.int32),
            pltpu.SMEM((CHUNKS, SHARDS), jnp.int32),
            pltpu.SemaphoreType.DMA((PARTS + 1,)),
            pltpu.SemaphoreType.DMA,
        ],
        compiler_params=pltpu.CompilerParams(vmem_limit_bytes=VMEM),
        name="cluster",
    )(pool)


def post_kernel(back_hbm, slot_ref, base_hbm, w_hbm, out_ref, back, base, weights, mix, sems):
    copies = []
    for index in range(HC // 2):
        span = pl.ds(index * 2 * REGION, 2 * REGION)
        copies.append(pltpu.make_async_copy(back_hbm.at[span], back.at[span], sems.at[index]))
    copies.append(
        pltpu.make_async_copy(w_hbm.at[pl.ds(HL * HD, HC * HD)], weights, sems.at[HC // 2])
    )
    copies.append(pltpu.make_async_copy(base_hbm, base, sems.at[HC // 2 + 1]))
    for copy in copies:
        copy.start()
    columns = iota((TOK, REGION), 1)
    for head in range(HC):
        if head % 2 == 0:
            copies[head // 2].wait()
        table = one_hot(columns == slot_ref[:, head : head + 1])
        mix[:, head * HD : (head + 1) * HD] = jnp.dot(
            table, back[head * REGION : (head + 1) * REGION, :], preferred_element_type=F32
        ).astype(BF16)
    copies[-2].wait()
    copies[-1].wait()
    for low in range(0, TOK, 256):
        rows = slice(low, low + 256)
        out_ref[rows, :] = (
            base[rows, :] + jnp.dot(mix[rows, :], weights[...], preferred_element_type=F32)
        ).astype(BF16)


def post_call(back, slot, base, w_output):
    return pl.pallas_call(
        post_kernel,
        in_specs=[
            pl.BlockSpec(memory_space=pl.ANY),
            pl.BlockSpec(memory_space=pltpu.VMEM),
            pl.BlockSpec(memory_space=pl.ANY),
            pl.BlockSpec(memory_space=pl.ANY),
        ],
        out_specs=pl.BlockSpec(memory_space=pltpu.VMEM),
        out_shape=jax.ShapeDtypeStruct((TOK, D), BF16),
        scratch_shapes=[
            pltpu.VMEM((HC * REGION, HD), BF16),
            pltpu.VMEM((TOK, D), F32),
            pltpu.VMEM((HC * HD, D), BF16),
            pltpu.VMEM((TOK, HC * HD), BF16),
            pltpu.SemaphoreType.DMA((HC // 2 + 2,)),
        ],
        compiler_params=pltpu.CompilerParams(vmem_limit_bytes=VMEM),
        name="collect",
    )(back, slot, base, w_output)


def token_slots(assignment):
    member = assignment[:, :, None] == jnp.arange(CLUSTERS, dtype=jnp.int32)
    rows = jnp.arange(TOK, dtype=jnp.int32)
    earlier = (rows[:, None] > rows[None, :]).astype(BF16)
    running = jnp.dot(
        earlier, member.astype(BF16).reshape(TOK, HC * CLUSTERS), preferred_element_type=F32
    ).reshape(TOK, HC, CLUSTERS)
    position = jnp.sum(jnp.where(member, running, 0.0), axis=2).astype(jnp.int32)
    return (assignment >> 1) * POOL + slot_of(assignment, position)


def body(activations, norm_gain, w_local, w_cluster, w_output, assignment):
    device = lax.axis_index(AXES)
    placed = pre_call(activations, norm_gain, w_cluster, assignment)
    got_pool = lax.all_to_all(placed, AXES, split_axis=0, concat_axis=0, tiled=True)

    local_qkv = jnp.dot(
        rms_norm(activations, norm_gain), w_local, preferred_element_type=F32
    ).astype(BF16)
    slot = token_slots(assignment)

    local_kv = local_qkv[:, HL * HD :]
    rim = lax.ppermute(local_kv, AXES, [(i, i + 1) for i in range(SHARDS - 1)])
    finished = cluster_call(got_pool)
    finished, rim = lax.optimization_barrier((finished, rim))
    came_back = lax.all_to_all(
        finished.reshape(SHARDS, POOL, HD), AXES, split_axis=0, concat_axis=0, tiled=True
    )
    base = window_call(
        jnp.minimum(device, 1).astype(jnp.int32).reshape(1), local_qkv, rim, activations, w_output
    )
    return post_call(came_back.reshape(SHARDS * POOL, HD), slot, base, w_output)


def solution(mesh):
    in_specs = (P(AXES, None), P(), P(), P(), P(), P(AXES, None))
    out_specs = P(AXES, None)
    return jax.shard_map(body, mesh=mesh, in_specs=in_specs, out_specs=out_specs, check_vma=False)
```

```python
import functools
import math

import jax
import jax.numpy as jnp
from jax import lax
from jax.experimental import pallas as pl
from jax.experimental.pallas import tpu as pltpu
from jax.sharding import PartitionSpec as P

HL = 4
HC = 8
HD = 128
WIN = 512
CSIZE = 2048
CLUSTERS = 32
TOK = 512
D = 1024
SHARDS = 128
POOL = 40
PER_CLUSTER = 28
GROUPS = CLUSTERS // 2
REGION = GROUPS * POOL
MAIN = 32
TAIL = POOL - MAIN
PACK = 3 * MAIN + 4 * TAIL
HEADS_STEP = 2
CHUNK = 4
CHUNKS = SHARDS // CHUNK
CHUNK_ROWS = CHUNK * POOL
SPAN = CHUNK * PER_CLUSTER + 16
QBLOCK = 1024
PARTS = 4
EPSILON = 1e-06
AXES = ("sx", "sy")
VMEM = 60 * 2**20
EXP2_SCALE = HD ** (-0.5) * math.log2(math.e)
NT = (((1,), (1,)), ((), ()))
TN = (((0,), (0,)), ((), ()))
F32 = jnp.float32
BF16 = jnp.bfloat16


def iota(shape, dim):
    return lax.broadcasted_iota(jnp.int32, shape, dim)


def one_hot(condition):
    return jnp.where(condition, 1.0, 0.0).astype(BF16)


def rms_norm(activations, norm_gain):
    values = activations.astype(F32)
    mean_square = jnp.mean(values * values, axis=-1, keepdims=True)
    return (values * lax.rsqrt(mean_square + EPSILON) * norm_gain).astype(BF16)


def slot_of(cluster, position):
    return jnp.where((cluster & 1) == 1, POOL - 1 - position, position)


def pre_kernel(
    act_hbm, gain_ref, w_hbm, asg_ref, out_hbm, act, weights, normed, rows, sizes, stage, arrived, leaving
):
    steps = HC // HEADS_STEP
    width = HEADS_STEP * 3 * HD
    copies = [
        pltpu.make_async_copy(
            w_hbm.at[:, pl.ds(step * width, width)], weights.at[step], arrived.at[step]
        )
        for step in range(steps)
    ]
    act_copy = pltpu.make_async_copy(act_hbm, act, arrived.at[steps])
    act_copy.start()
    for copy in copies:
        copy.start()

    cluster = asg_ref[...]
    spread = one_hot((iota((HC * CLUSTERS, HC), 0) >> 5) == iota((HC * CLUSTERS, HC), 1))
    value = jnp.dot(spread, cluster.astype(F32).astype(BF16), preferred_element_type=F32)
    member = value == (iota((HC * CLUSTERS, TOK), 0) & (CLUSTERS - 1)).astype(F32)
    before = one_hot(iota((TOK, TOK), 0) < iota((TOK, TOK), 1))
    running = jnp.dot(one_hot(member), before, preferred_element_type=F32)
    gather = one_hot(iota((HC, HC * CLUSTERS), 0) == (iota((HC, HC * CLUSTERS), 1) >> 5))
    position = jnp.dot(
        gather, jnp.where(member, running, 0.0).astype(BF16), preferred_element_type=F32
    ).astype(jnp.int32)
    slot = slot_of(cluster, position)
    group = cluster >> 1
    rows[...] = jnp.where(
        slot < MAIN, group * MAIN + slot, GROUPS * MAIN + group * TAIL + slot - MAIN
    )
    sizes[...] = jnp.dot(
        one_hot(member), jnp.ones((TOK, HD), BF16), preferred_element_type=F32
    ).astype(BF16)
    which = iota((GROUPS * TAIL, CLUSTERS), 0)
    pick = one_hot(
        ((which >> 3) * 2 + (which & 7) == iota((GROUPS * TAIL, CLUSTERS), 1)) & ((which & 7) < 2)
    )
    act_copy.wait()
    normed[...] = rms_norm(act[...], gain_ref[...])

    def project(step):
        copies[step].wait()
        return jnp.dot(normed[...], weights[step], preferred_element_type=F32).astype(BF16)

    sent = []
    qkv = project(0)
    for step in range(steps):
        later = project(step + 1) if step + 1 < steps else None
        for inner in range(HEADS_STEP):
            head = step * HEADS_STEP + inner
            table = one_hot(iota((REGION, TOK), 0) == rows[head : head + 1, :])
            placed = jnp.dot(
                table, qkv[:, inner * 3 * HD : (inner + 1) * 3 * HD], preferred_element_type=F32
            )
            groups = slice(head * GROUPS, (head + 1) * GROUPS)
            tails = []
            for kind in range(3):
                part = placed[:, kind * HD : (kind + 1) * HD]
                stage[groups, kind * MAIN : (kind + 1) * MAIN, :] = (
                    part[: GROUPS * MAIN].astype(BF16).reshape(GROUPS, MAIN, HD)
                )
                tails.append(part[GROUPS * MAIN :].reshape(GROUPS, TAIL, HD))
            size = sizes[head * CLUSTERS : (head + 1) * CLUSTERS, :]
            tails.append(
                jnp.dot(pick, size, preferred_element_type=F32).reshape(GROUPS, TAIL, HD)
            )
            stage[groups, 3 * MAIN :, :] = jnp.concatenate(tails, axis=1).astype(BF16)
        span = pl.ds(step * HEADS_STEP * GROUPS, HEADS_STEP * GROUPS)
        sent.append(pltpu.make_async_copy(stage.at[span], out_hbm.at[span], leaving.at[step]))
        sent[step].start()
        qkv = later
    for copy in sent:
        copy.wait()


def pre_call(activations, norm_gain, w_cluster, assignment):
    steps = HC // HEADS_STEP
    return pl.pallas_call(
        pre_kernel,
        in_specs=[
            pl.BlockSpec(memory_space=pl.ANY),
            pl.BlockSpec(memory_space=pltpu.VMEM),
            pl.BlockSpec(memory_space=pl.ANY),
            pl.BlockSpec(memory_space=pltpu.VMEM),
        ],
        out_specs=pl.BlockSpec(memory_space=pl.ANY),
        out_shape=jax.ShapeDtypeStruct((SHARDS, PACK, HD), BF16),
        scratch_shapes=[
            pltpu.VMEM((TOK, D), BF16),
            pltpu.VMEM((steps, D, HEADS_STEP * 3 * HD), BF16),
            pltpu.VMEM((TOK, D), BF16),
            pltpu.VMEM((HC, TOK), jnp.int32),
            pltpu.VMEM((HC * CLUSTERS, HD), BF16),
            pltpu.VMEM((SHARDS, PACK, HD), BF16),
            pltpu.SemaphoreType.DMA((steps + 1,)),
            pltpu.SemaphoreType.DMA((steps,)),
        ],
        compiler_params=pltpu.CompilerParams(vmem_limit_bytes=VMEM),
        name="place",
    )(activations, norm_gain.reshape(1, D), w_cluster, assignment.T)


def softmax_rows(scores):
    highest = jnp.max(scores, axis=-1, keepdims=True)
    raised = jnp.exp2((scores - highest) * EXP2_SCALE)
    total = jnp.sum(raised, axis=-1, keepdims=True)
    return (raised * (1.0 / total)).astype(BF16)


def window_kernel(first_ref, qkv_ref, rim_ref, act_ref, w_ref, out_ref, mix):
    width = HL * HD
    step = 128
    shift = jnp.where(first_ref[0] == 0, WIN, 0)
    for head in range(HL):
        lanes = slice(head * HD, (head + 1) * HD)
        key_lanes = slice(width + head * HD, width + (head + 1) * HD)
        value_lanes = slice(2 * width + head * HD, 2 * width + (head + 1) * HD)
        for low in range(0, TOK, step):
            high = low + step
            query = qkv_ref[low:high, lanes]
            keys = jnp.concatenate([rim_ref[low:, lanes], qkv_ref[:high, key_lanes]], axis=0)
            values = jnp.concatenate(
                [rim_ref[low:, key_lanes], qkv_ref[:high, value_lanes]], axis=0
            )
            scores = lax.dot_general(query, keys, NT, preferred_element_type=F32)
            rows = iota(scores.shape, 0)
            cols = iota(scores.shape, 1)
            allowed = (cols > rows) & (cols <= rows + WIN) & (cols + low >= shift)
            weights = softmax_rows(jnp.where(allowed, scores, -1e30))
            mix[low:high, lanes] = jnp.dot(weights, values, preferred_element_type=F32).astype(BF16)
    out_ref[...] = act_ref[...].astype(F32) + jnp.dot(
        mix[...], w_ref[...], preferred_element_type=F32
    )


def window_call(first, local_qkv, rim, activations, w_output):
    width = HL * HD
    return pl.pallas_call(
        window_kernel,
        grid=(1,),
        in_specs=[
            pl.BlockSpec(memory_space=pltpu.SMEM),
            pl.BlockSpec((TOK, 3 * width), lambda i: (0, 0)),
            pl.BlockSpec((WIN, 2 * width), lambda i: (0, 0)),
            pl.BlockSpec((TOK, D), lambda i: (0, 0)),
            pl.BlockSpec((width, D), lambda i: (0, 0)),
        ],
        out_specs=pl.BlockSpec((TOK, D), lambda i: (0, 0)),
        out_shape=jax.ShapeDtypeStruct((TOK, D), F32),
        scratch_shapes=[pltpu.VMEM((TOK, width), BF16)],
        compiler_params=pltpu.CompilerParams(vmem_limit_bytes=VMEM),
        cost_estimate=pl.CostEstimate(flops=10**10, bytes_accessed=10**7, transcendentals=0),
        name="window",
    )(first, local_qkv, rim, activations, w_output)


def plan_moves(meta, main_rows, tail_rows, back_rows, first_rows):
    source = iota((SHARDS, SHARDS), 0)
    other = iota((SHARDS, SHARDS), 1)
    earlier = one_hot(other < source)
    chunk_earlier = one_hot(other < (source & ~(CHUNK - 1)))
    own_lanes = [(source & (CHUNK - 1)) == (other >> shift) for shift in (5, 3)]
    chunk_of = one_hot(iota((CHUNKS, SHARDS), 0) == (iota((CHUNKS, SHARDS), 1) >> 2))
    leader = one_hot(iota((CHUNKS, SHARDS), 0) * CHUNK == iota((CHUNKS, SHARDS), 1))
    lane = iota((CHUNKS, SHARDS), 1)
    tail_block = meta[...].reshape(SHARDS * 16, HD)
    picked = iota((SHARDS, SHARDS * 16), 1) - iota((SHARDS, SHARDS * 16), 0) * 16

    def by_chunk(values, own):
        return jnp.dot(
            chunk_of, jnp.where(own, values, 0.0).astype(BF16), preferred_element_type=F32
        ).astype(jnp.int32)

    starts, sizes, firsts = [], [], []
    for which in range(2):
        size = jnp.dot(
            one_hot(picked == 8 + which), tail_block, preferred_element_type=F32
        ).astype(BF16)
        start = jnp.dot(earlier, size, preferred_element_type=F32).astype(jnp.int32)
        first = jnp.dot(chunk_earlier, size, preferred_element_type=F32).astype(jnp.int32) >> 4
        local = (start - (first << 4)).astype(F32)
        starts.append([by_chunk(local, own) for own in own_lanes])
        sizes.append([by_chunk(size.astype(F32), own) for own in own_lanes])
        firsts.append(
            jnp.dot(leader, first.astype(F32).astype(BF16), preferred_element_type=F32).astype(
                jnp.int32
            )
            << 4
        )

    def moves(slot, table):
        last = POOL - 1 - slot
        return jnp.where(
            slot < sizes[0][table],
            starts[0][table] + slot,
            jnp.where(last < sizes[1][table], SPAN + starts[1][table] + last, -1),
        )

    main = moves(lane & (MAIN - 1), 0)
    tail = moves(MAIN + (lane & (TAIL - 1)), 1)
    main_rows[...] = main
    tail_rows[...] = tail
    back_rows[...] = (
        jnp.concatenate(
            [
                main.astype(F32).T.reshape(CHUNK, MAIN, CHUNKS),
                tail.astype(F32).T[: CHUNK * TAIL].reshape(CHUNK, TAIL, CHUNKS),
            ],
            axis=1,
        )
        .reshape(CHUNK_ROWS, CHUNKS)
        .astype(BF16)
    )
    first_rows[...] = jnp.where(iota((CHUNKS, SHARDS), 1) == 0, firsts[0], firsts[1])


def cluster_kernel(
    pool_hbm,
    out_hbm,
    pool,
    meta,
    packed,
    mixed,
    scores,
    tops,
    turned,
    main_rows,
    tail_rows,
    back_rows,
    first_rows,
    firsts,
    arrived,
    planned,
    result,
    leaving,
):
    part = SHARDS // PARTS
    head_copy = pltpu.make_async_copy(pool_hbm.at[:, PACK - 16 :, :], meta, arrived.at[PARTS])
    head_copy.start()
    copies = []
    for index in range(PARTS):
        span = pl.ds(index * part, part)
        copies.append(pltpu.make_async_copy(pool_hbm.at[span], pool.at[span], arrived.at[index]))
        copies[index].start()
    packed[:, :, :16] = jnp.zeros((3, 2, 16, HD), BF16)
    mixed[:, CSIZE:] = jnp.zeros((2, SPAN, HD), BF16)
    head_copy.wait()
    plan_moves(meta, main_rows, tail_rows, back_rows, first_rows)
    plan_copy = pltpu.make_async_copy(first_rows, firsts, planned)
    plan_copy.start()
    plan_copy.wait()
    row_ids = iota((2 * SPAN, SHARDS), 0)

    def compact(chunk):
        here = pl.ds(chunk, 1)
        sources = pl.ds(chunk * CHUNK, CHUNK)
        table = jnp.concatenate(
            [
                one_hot(row_ids == main_rows[here, :]),
                one_hot(row_ids == tail_rows[here, :])[:, : CHUNK * TAIL],
            ],
            axis=1,
        )
        tail = pool[sources, 3 * MAIN :, :].astype(F32)
        kinds = []
        for kind in range(3):
            rows = pool[sources, kind * MAIN : (kind + 1) * MAIN, :].reshape(CHUNK * MAIN, HD)
            more = tail[:, kind * TAIL : (kind + 1) * TAIL].reshape(CHUNK * TAIL, HD)
            kinds.append(jnp.concatenate([rows, more.astype(BF16)], axis=0))
        moved = jnp.dot(
            table, jnp.concatenate(kinds, axis=1), preferred_element_type=F32
        ).astype(BF16)
        for which in range(2):
            first = pl.multiple_of(firsts[chunk, which], 16)
            rest = pl.ds(pl.multiple_of(first + 16, 16), SPAN - 16)
            for kind in range(3):
                rows = moved[which * SPAN : (which + 1) * SPAN, kind * HD : (kind + 1) * HD]
                packed[kind, which, pl.ds(first, 16), :] += rows[:16]
                packed[kind, which, rest, :] = rows[16:]

    for index in range(PARTS):
        copies[index].wait()
        pl.loop(index * CHUNKS // PARTS, (index + 1) * CHUNKS // PARTS, unroll=8)(compact)

    for which in range(2):
        for low in range(0, CSIZE, 256):
            turned[which, :, low : low + 256] = packed[2, which, low : low + 256, :].T

    blocks = CSIZE // QBLOCK

    def score(buffer, index):
        which = index // blocks
        place = pl.ds(pl.multiple_of(index % blocks * QBLOCK, QBLOCK), QBLOCK)
        values = lax.dot_general(
            packed[1, which, :CSIZE, :],
            packed[0, which, place, :],
            NT,
            preferred_element_type=F32,
        )
        scores[buffer] = values
        tops[buffer] = jnp.max(values, axis=0, keepdims=True)

    score(0, 0)

    @pl.loop(0, 2 * blocks, step=2)
    def _(pair):
        for inner in range(2):
            index = pair + inner
            which = index // blocks
            place = pl.ds(pl.multiple_of(index % blocks * QBLOCK, QBLOCK), QBLOCK)
            score(1 - inner, jnp.minimum(index + 1, 2 * blocks - 1))
            raised = jnp.exp2((scores[inner] - tops[inner]) * EXP2_SCALE)
            scale = 1.0 / jnp.sum(raised, axis=0, keepdims=True)
            weights = (raised * scale).astype(BF16)
            mix = jnp.dot(turned[which], weights, preferred_element_type=F32)
            mixed[which, place, :] = mix.T.astype(BF16)

    columns = iota((CHUNK_ROWS, 2 * SPAN), 1).astype(F32)
    group = CHUNKS // PARTS
    sent = []
    for index in range(PARTS):
        lanes = iota((CHUNKS, group * 2 * SPAN), 1)
        spread = one_hot(iota((CHUNKS, group * 2 * SPAN), 0) == index * group + (lanes >> 8))
        target = jnp.dot(back_rows[...], spread, preferred_element_type=F32)
        for inner in range(group):
            chunk = index * group + inner
            table = one_hot(target[:, inner * 2 * SPAN : (inner + 1) * 2 * SPAN] == columns)
            rows = jnp.concatenate(
                [
                    mixed[which, pl.ds(pl.multiple_of(firsts[chunk, which], 16), SPAN), :]
                    for which in range(2)
                ],
                axis=0,
            )
            result[chunk * CHUNK_ROWS : (chunk + 1) * CHUNK_ROWS, :] = jnp.dot(
                table, rows, preferred_element_type=F32
            ).astype(BF16)
        span = pl.ds(index * group * CHUNK_ROWS, group * CHUNK_ROWS)
        sent.append(pltpu.make_async_copy(result.at[span], out_hbm.at[span], leaving.at[index]))
        sent[index].start()
    for copy in sent:
        copy.wait()


def cluster_call(pool):
    return pl.pallas_call(
        cluster_kernel,
        in_specs=[pl.BlockSpec(memory_space=pl.ANY)],
        out_specs=pl.BlockSpec(memory_space=pl.ANY),
        out_shape=jax.ShapeDtypeStruct((SHARDS * POOL, HD), BF16),
        scratch_shapes=[
            pltpu.VMEM((SHARDS, PACK, HD), BF16),
            pltpu.VMEM((SHARDS, 16, HD), BF16),
            pltpu.VMEM((3, 2, CSIZE + SPAN, HD), BF16),
            pltpu.VMEM((2, CSIZE + SPAN, HD), BF16),
            pltpu.VMEM((2, CSIZE, QBLOCK), F32),
            pltpu.VMEM((2, 1, QBLOCK), F32),
            pltpu.VMEM((2, HD, CSIZE), BF16),
            pltpu.VMEM((CHUNKS, SHARDS), jnp.int32),
            pltpu.VMEM((CHUNKS, SHARDS), jnp.int32),
            pltpu.VMEM((CHUNK_ROWS, CHUNKS), BF16),
            pltpu.VMEM((CHUNKS, SHARDS), jnp.int32),
            pltpu.SMEM((CHUNKS, SHARDS), jnp.int32),
            pltpu.SemaphoreType.DMA((PARTS + 1,)),
            pltpu.SemaphoreType.DMA,
            pltpu.VMEM((SHARDS * POOL, HD), BF16),
            pltpu.SemaphoreType.DMA((PARTS,)),
        ],
        compiler_params=pltpu.CompilerParams(vmem_limit_bytes=VMEM),
        name="cluster",
    )(pool)


def post_kernel(back_hbm, slot_ref, base_hbm, w_hbm, out_ref, back, base, weights, mix, sems):
    copies = []
    for index in range(HC // 2):
        span = pl.ds(index * 2 * REGION, 2 * REGION)
        copies.append(pltpu.make_async_copy(back_hbm.at[span], back.at[span], sems.at[index]))
    copies.append(
        pltpu.make_async_copy(w_hbm.at[pl.ds(HL * HD, HC * HD)], weights, sems.at[HC // 2])
    )
    copies.append(pltpu.make_async_copy(base_hbm, base, sems.at[HC // 2 + 1]))
    for copy in copies:
        copy.start()
    columns = iota((TOK, REGION), 1)
    for head in range(HC):
        if head % 2 == 0:
            copies[head // 2].wait()
        table = one_hot(columns == slot_ref[:, head : head + 1])
        mix[:, head * HD : (head + 1) * HD] = jnp.dot(
            table, back[head * REGION : (head + 1) * REGION, :], preferred_element_type=F32
        ).astype(BF16)
    copies[-2].wait()
    copies[-1].wait()
    for low in range(0, TOK, 256):
        rows = slice(low, low + 256)
        out_ref[rows, :] = (
            base[rows, :] + jnp.dot(mix[rows, :], weights[...], preferred_element_type=F32)
        ).astype(BF16)


def post_call(back, slot, base, w_output):
    return pl.pallas_call(
        post_kernel,
        in_specs=[
            pl.BlockSpec(memory_space=pl.ANY),
            pl.BlockSpec(memory_space=pltpu.VMEM),
            pl.BlockSpec(memory_space=pl.ANY),
            pl.BlockSpec(memory_space=pl.ANY),
        ],
        out_specs=pl.BlockSpec(memory_space=pltpu.VMEM),
        out_shape=jax.ShapeDtypeStruct((TOK, D), BF16),
        scratch_shapes=[
            pltpu.VMEM((HC * REGION, HD), BF16),
            pltpu.VMEM((TOK, D), F32),
            pltpu.VMEM((HC * HD, D), BF16),
            pltpu.VMEM((TOK, HC * HD), BF16),
            pltpu.SemaphoreType.DMA((HC // 2 + 2,)),
        ],
        compiler_params=pltpu.CompilerParams(vmem_limit_bytes=VMEM),
        name="collect",
    )(back, slot, base, w_output)


def token_slots(assignment):
    member = assignment[:, :, None] == jnp.arange(CLUSTERS, dtype=jnp.int32)
    rows = jnp.arange(TOK, dtype=jnp.int32)
    earlier = (rows[:, None] > rows[None, :]).astype(BF16)
    running = jnp.dot(
        earlier, member.astype(BF16).reshape(TOK, HC * CLUSTERS), preferred_element_type=F32
    ).reshape(TOK, HC, CLUSTERS)
    position = jnp.sum(jnp.where(member, running, 0.0), axis=2).astype(jnp.int32)
    return (assignment >> 1) * POOL + slot_of(assignment, position)


def body(activations, norm_gain, w_local, w_cluster, w_output, assignment):
    device = lax.axis_index(AXES)
    placed = pre_call(activations, norm_gain, w_cluster, assignment)
    got_pool = lax.all_to_all(placed, AXES, split_axis=0, concat_axis=0, tiled=True)

    local_qkv = jnp.dot(
        rms_norm(activations, norm_gain), w_local, preferred_element_type=F32
    ).astype(BF16)
    slot = token_slots(assignment)

    local_kv = local_qkv[:, HL * HD :]
    rim = lax.ppermute(local_kv, AXES, [(i, i + 1) for i in range(SHARDS - 1)])
    finished = cluster_call(got_pool)
    finished, rim = lax.optimization_barrier((finished, rim))
    came_back = lax.all_to_all(
        finished.reshape(SHARDS, POOL, HD), AXES, split_axis=0, concat_axis=0, tiled=True
    )
    base = window_call(
        jnp.minimum(device, 1).astype(jnp.int32).reshape(1), local_qkv, rim, activations, w_output
    )
    return post_call(came_back.reshape(SHARDS * POOL, HD), slot, base, w_output)


def solution(mesh):
    in_specs = (P(AXES, None), P(), P(), P(), P(), P(AXES, None))
    out_specs = P(AXES, None)
    return jax.shard_map(body, mesh=mesh, in_specs=in_specs, out_specs=out_specs, check_vma=False)
```

```python
import functools
import math

import jax
import jax.numpy as jnp
from jax import lax
from jax.experimental import pallas as pl
from jax.experimental.pallas import tpu as pltpu
from jax.sharding import PartitionSpec as P

HL = 4
HC = 8
HD = 128
WIN = 512
CSIZE = 2048
CLUSTERS = 32
TOK = 512
D = 1024
SHARDS = 128
POOL = 40
PER_CLUSTER = 28
GROUPS = CLUSTERS // 2
REGION = GROUPS * POOL
MAIN = 32
TAIL = POOL - MAIN
PACK = 3 * MAIN + 4 * TAIL
HEADS_STEP = 2
CHUNK = 4
CHUNKS = SHARDS // CHUNK
CHUNK_ROWS = CHUNK * POOL
SPAN = CHUNK * PER_CLUSTER + 16
QBLOCK = 1024
PARTS = 4
EPSILON = 1e-06
AXES = ("sx", "sy")
VMEM = 60 * 2**20
EXP2_SCALE = HD ** (-0.5) * math.log2(math.e)
NT = (((1,), (1,)), ((), ()))
TN = (((0,), (0,)), ((), ()))
F32 = jnp.float32
BF16 = jnp.bfloat16


def iota(shape, dim):
    return lax.broadcasted_iota(jnp.int32, shape, dim)


def one_hot(condition):
    return jnp.where(condition, 1.0, 0.0).astype(BF16)


def rms_norm(activations, norm_gain):
    values = activations.astype(F32)
    mean_square = jnp.mean(values * values, axis=-1, keepdims=True)
    return (values * lax.rsqrt(mean_square + EPSILON) * norm_gain).astype(BF16)


def slot_of(cluster, position):
    return jnp.where((cluster & 1) == 1, POOL - 1 - position, position)


def pre_kernel(
    act_hbm, gain_ref, w_hbm, asg_ref, out_hbm, act, weights, normed, rows, sizes, stage, arrived, leaving
):
    steps = HC // HEADS_STEP
    width = HEADS_STEP * 3 * HD
    copies = [
        pltpu.make_async_copy(
            w_hbm.at[:, pl.ds(step * width, width)], weights.at[step], arrived.at[step]
        )
        for step in range(steps)
    ]
    act_copy = pltpu.make_async_copy(act_hbm, act, arrived.at[steps])
    act_copy.start()
    for copy in copies:
        copy.start()

    cluster = asg_ref[...]
    spread = one_hot((iota((HC * CLUSTERS, HC), 0) >> 5) == iota((HC * CLUSTERS, HC), 1))
    value = jnp.dot(spread, cluster.astype(F32).astype(BF16), preferred_element_type=F32)
    member = value == (iota((HC * CLUSTERS, TOK), 0) & (CLUSTERS - 1)).astype(F32)
    before = one_hot(iota((TOK, TOK), 0) < iota((TOK, TOK), 1))
    running = jnp.dot(one_hot(member), before, preferred_element_type=F32)
    gather = one_hot(iota((HC, HC * CLUSTERS), 0) == (iota((HC, HC * CLUSTERS), 1) >> 5))
    position = jnp.dot(
        gather, jnp.where(member, running, 0.0).astype(BF16), preferred_element_type=F32
    ).astype(jnp.int32)
    slot = slot_of(cluster, position)
    group = cluster >> 1
    rows[...] = jnp.where(
        slot < MAIN, group * MAIN + slot, GROUPS * MAIN + group * TAIL + slot - MAIN
    )
    sizes[...] = jnp.dot(
        one_hot(member), jnp.ones((TOK, HD), BF16), preferred_element_type=F32
    ).astype(BF16)
    which = iota((GROUPS * TAIL, CLUSTERS), 0)
    pick = one_hot(
        ((which >> 3) * 2 + (which & 7) == iota((GROUPS * TAIL, CLUSTERS), 1)) & ((which & 7) < 2)
    )
    act_copy.wait()
    normed[...] = rms_norm(act[...], gain_ref[...])

    def project(step):
        copies[step].wait()
        return jnp.dot(normed[...], weights[step], preferred_element_type=F32).astype(BF16)

    sent = []
    qkv = project(0)
    for step in range(steps):
        later = project(step + 1) if step + 1 < steps else None
        for inner in range(HEADS_STEP):
            head = step * HEADS_STEP + inner
            table = one_hot(iota((REGION, TOK), 0) == rows[head : head + 1, :])
            placed = jnp.dot(
                table, qkv[:, inner * 3 * HD : (inner + 1) * 3 * HD], preferred_element_type=F32
            )
            groups = slice(head * GROUPS, (head + 1) * GROUPS)
            tails = []
            for kind in range(3):
                part = placed[:, kind * HD : (kind + 1) * HD]
                stage[groups, kind * MAIN : (kind + 1) * MAIN, :] = (
                    part[: GROUPS * MAIN].astype(BF16).reshape(GROUPS, MAIN, HD)
                )
                tails.append(part[GROUPS * MAIN :].reshape(GROUPS, TAIL, HD))
            size = sizes[head * CLUSTERS : (head + 1) * CLUSTERS, :]
            tails.append(
                jnp.dot(pick, size, preferred_element_type=F32).reshape(GROUPS, TAIL, HD)
            )
            stage[groups, 3 * MAIN :, :] = jnp.concatenate(tails, axis=1).astype(BF16)
        span = pl.ds(step * HEADS_STEP * GROUPS, HEADS_STEP * GROUPS)
        sent.append(pltpu.make_async_copy(stage.at[span], out_hbm.at[span], leaving.at[step]))
        sent[step].start()
        qkv = later
    for copy in sent:
        copy.wait()


def pre_call(activations, norm_gain, w_cluster, assignment):
    steps = HC // HEADS_STEP
    return pl.pallas_call(
        pre_kernel,
        in_specs=[
            pl.BlockSpec(memory_space=pl.ANY),
            pl.BlockSpec(memory_space=pltpu.VMEM),
            pl.BlockSpec(memory_space=pl.ANY),
            pl.BlockSpec(memory_space=pltpu.VMEM),
        ],
        out_specs=pl.BlockSpec(memory_space=pl.ANY),
        out_shape=jax.ShapeDtypeStruct((SHARDS, PACK, HD), BF16),
        scratch_shapes=[
            pltpu.VMEM((TOK, D), BF16),
            pltpu.VMEM((steps, D, HEADS_STEP * 3 * HD), BF16),
            pltpu.VMEM((TOK, D), BF16),
            pltpu.VMEM((HC, TOK), jnp.int32),
            pltpu.VMEM((HC * CLUSTERS, HD), BF16),
            pltpu.VMEM((SHARDS, PACK, HD), BF16),
            pltpu.SemaphoreType.DMA((steps + 1,)),
            pltpu.SemaphoreType.DMA((steps,)),
        ],
        compiler_params=pltpu.CompilerParams(vmem_limit_bytes=VMEM),
        name="place",
    )(activations, norm_gain.reshape(1, D), w_cluster, assignment.T)


def softmax_rows(scores):
    highest = jnp.max(scores, axis=-1, keepdims=True)
    raised = jnp.exp2((scores - highest) * EXP2_SCALE)
    total = jnp.sum(raised, axis=-1, keepdims=True)
    return (raised * (1.0 / total)).astype(BF16)


def window_kernel(first_ref, qkv_ref, rim_ref, act_ref, w_ref, out_ref, mix):
    width = HL * HD
    step = 128
    shift = jnp.where(first_ref[0] == 0, WIN, 0)
    for head in range(HL):
        lanes = slice(head * HD, (head + 1) * HD)
        key_lanes = slice(width + head * HD, width + (head + 1) * HD)
        value_lanes = slice(2 * width + head * HD, 2 * width + (head + 1) * HD)
        for low in range(0, TOK, step):
            high = low + step
            query = qkv_ref[low:high, lanes]
            keys = jnp.concatenate([rim_ref[low:, lanes], qkv_ref[:high, key_lanes]], axis=0)
            values = jnp.concatenate(
                [rim_ref[low:, key_lanes], qkv_ref[:high, value_lanes]], axis=0
            )
            scores = lax.dot_general(query, keys, NT, preferred_element_type=F32)
            rows = iota(scores.shape, 0)
            cols = iota(scores.shape, 1)
            allowed = (cols > rows) & (cols <= rows + WIN) & (cols + low >= shift)
            weights = softmax_rows(jnp.where(allowed, scores, -1e30))
            mix[low:high, lanes] = jnp.dot(weights, values, preferred_element_type=F32).astype(BF16)
    out_ref[...] = act_ref[...].astype(F32) + jnp.dot(
        mix[...], w_ref[...], preferred_element_type=F32
    )


def window_call(first, local_qkv, rim, activations, w_output):
    width = HL * HD
    return pl.pallas_call(
        window_kernel,
        grid=(1,),
        in_specs=[
            pl.BlockSpec(memory_space=pltpu.SMEM),
            pl.BlockSpec((TOK, 3 * width), lambda i: (0, 0)),
            pl.BlockSpec((WIN, 2 * width), lambda i: (0, 0)),
            pl.BlockSpec((TOK, D), lambda i: (0, 0)),
            pl.BlockSpec((width, D), lambda i: (0, 0)),
        ],
        out_specs=pl.BlockSpec((TOK, D), lambda i: (0, 0)),
        out_shape=jax.ShapeDtypeStruct((TOK, D), F32),
        scratch_shapes=[pltpu.VMEM((TOK, width), BF16)],
        compiler_params=pltpu.CompilerParams(vmem_limit_bytes=VMEM),
        cost_estimate=pl.CostEstimate(flops=10**10, bytes_accessed=10**7, transcendentals=0),
        name="window",
    )(first, local_qkv, rim, activations, w_output)


def plan_moves(meta, main_rows, tail_rows, back_rows, first_rows):
    source = iota((SHARDS, SHARDS), 0)
    other = iota((SHARDS, SHARDS), 1)
    earlier = one_hot(other < source)
    chunk_earlier = one_hot(other < (source & ~(CHUNK - 1)))
    own_lanes = [(source & (CHUNK - 1)) == (other >> shift) for shift in (5, 3)]
    chunk_of = one_hot(iota((CHUNKS, SHARDS), 0) == (iota((CHUNKS, SHARDS), 1) >> 2))
    leader = one_hot(iota((CHUNKS, SHARDS), 0) * CHUNK == iota((CHUNKS, SHARDS), 1))
    lane = iota((CHUNKS, SHARDS), 1)
    tail_block = meta[...].reshape(SHARDS * 16, HD)
    picked = iota((SHARDS, SHARDS * 16), 1) - iota((SHARDS, SHARDS * 16), 0) * 16

    def by_chunk(values, own):
        return jnp.dot(
            chunk_of, jnp.where(own, values, 0.0).astype(BF16), preferred_element_type=F32
        ).astype(jnp.int32)

    starts, sizes, firsts = [], [], []
    for which in range(2):
        size = jnp.dot(
            one_hot(picked == 8 + which), tail_block, preferred_element_type=F32
        ).astype(BF16)
        start = jnp.dot(earlier, size, preferred_element_type=F32).astype(jnp.int32)
        first = jnp.dot(chunk_earlier, size, preferred_element_type=F32).astype(jnp.int32) >> 4
        local = (start - (first << 4)).astype(F32)
        starts.append([by_chunk(local, own) for own in own_lanes])
        sizes.append([by_chunk(size.astype(F32), own) for own in own_lanes])
        firsts.append(
            jnp.dot(leader, first.astype(F32).astype(BF16), preferred_element_type=F32).astype(
                jnp.int32
            )
            << 4
        )

    def moves(slot, table):
        last = POOL - 1 - slot
        return jnp.where(
            slot < sizes[0][table],
            starts[0][table] + slot,
            jnp.where(last < sizes[1][table], SPAN + starts[1][table] + last, -1),
        )

    main = moves(lane & (MAIN - 1), 0)
    tail = moves(MAIN + (lane & (TAIL - 1)), 1)
    main_rows[...] = main
    tail_rows[...] = tail
    back_rows[...] = (
        jnp.concatenate(
            [
                main.astype(F32).T.reshape(CHUNK, MAIN, CHUNKS),
                tail.astype(F32).T[: CHUNK * TAIL].reshape(CHUNK, TAIL, CHUNKS),
            ],
            axis=1,
        )
        .reshape(CHUNK_ROWS, CHUNKS)
        .astype(BF16)
    )
    first_rows[...] = jnp.where(iota((CHUNKS, SHARDS), 1) == 0, firsts[0], firsts[1])


def cluster_kernel(
    pool_hbm,
    out_hbm,
    pool,
    meta,
    packed,
    mixed,
    scores,
    tops,
    turned,
    main_rows,
    tail_rows,
    back_rows,
    first_rows,
    firsts,
    arrived,
    planned,
    result,
    leaving,
):
    part = SHARDS // PARTS
    head_copy = pltpu.make_async_copy(pool_hbm.at[:, PACK - 16 :, :], meta, arrived.at[PARTS])
    head_copy.start()
    copies = []
    for index in range(PARTS):
        span = pl.ds(index * part, part)
        copies.append(pltpu.make_async_copy(pool_hbm.at[span], pool.at[span], arrived.at[index]))
        copies[index].start()
    packed[:, :, :16] = jnp.zeros((3, 2, 16, HD), BF16)
    mixed[:, CSIZE:] = jnp.zeros((2, SPAN, HD), BF16)
    head_copy.wait()
    plan_moves(meta, main_rows, tail_rows, back_rows, first_rows)
    plan_copy = pltpu.make_async_copy(first_rows, firsts, planned)
    plan_copy.start()
    plan_copy.wait()
    row_ids = iota((2 * SPAN, SHARDS), 0)

    def compact(chunk):
        here = pl.ds(chunk, 1)
        sources = pl.ds(chunk * CHUNK, CHUNK)
        table = jnp.concatenate(
            [
                one_hot(row_ids == main_rows[here, :]),
                one_hot(row_ids == tail_rows[here, :])[:, : CHUNK * TAIL],
            ],
            axis=1,
        )
        tail = pool[sources, 3 * MAIN :, :].astype(F32)
        kinds = []
        for kind in range(3):
            rows = pool[sources, kind * MAIN : (kind + 1) * MAIN, :].reshape(CHUNK * MAIN, HD)
            more = tail[:, kind * TAIL : (kind + 1) * TAIL].reshape(CHUNK * TAIL, HD)
            kinds.append(jnp.concatenate([rows, more.astype(BF16)], axis=0))
        moved = jnp.dot(
            table, jnp.concatenate(kinds, axis=1), preferred_element_type=F32
        ).astype(BF16)
        for which in range(2):
            first = pl.multiple_of(firsts[chunk, which], 16)
            rest = pl.ds(pl.multiple_of(first + 16, 16), SPAN - 16)
            for kind in range(3):
                rows = moved[which * SPAN : (which + 1) * SPAN, kind * HD : (kind + 1) * HD]
                packed[kind, which, pl.ds(first, 16), :] += rows[:16]
                packed[kind, which, rest, :] = rows[16:]

    for index in range(PARTS):
        copies[index].wait()
        pl.loop(index * CHUNKS // PARTS, (index + 1) * CHUNKS // PARTS, unroll=8)(compact)

    for which in range(2):
        for low in range(0, CSIZE, 256):
            turned[which, :, low : low + 256] = packed[2, which, low : low + 256, :].T

    blocks = CSIZE // QBLOCK

    def score(buffer, index):
        which = index // blocks
        place = pl.ds(pl.multiple_of(index % blocks * QBLOCK, QBLOCK), QBLOCK)
        values = lax.dot_general(
            packed[1, which, :CSIZE, :],
            packed[0, which, place, :],
            NT,
            preferred_element_type=F32,
        )
        scores[buffer] = values
        tops[buffer] = jnp.max(values, axis=0, keepdims=True)

    score(0, 0)

    @pl.loop(0, 2 * blocks, step=2)
    def _(pair):
        for inner in range(2):
            index = pair + inner
            which = index // blocks
            place = pl.ds(pl.multiple_of(index % blocks * QBLOCK, QBLOCK), QBLOCK)
            score(1 - inner, jnp.minimum(index + 1, 2 * blocks - 1))
            raised = jnp.exp2((scores[inner] - tops[inner]) * EXP2_SCALE)
            scale = 1.0 / jnp.sum(raised, axis=0, keepdims=True)
            weights = (raised * scale).astype(BF16)
            mix = jnp.dot(turned[which], weights, preferred_element_type=F32)
            mixed[which, place, :] = mix.T.astype(BF16)

    columns = iota((CHUNK_ROWS, 2 * SPAN), 1).astype(F32)
    group = CHUNKS // PARTS
    sent = []
    for index in range(PARTS):
        lanes = iota((CHUNKS, group * 2 * SPAN), 1)
        spread = one_hot(iota((CHUNKS, group * 2 * SPAN), 0) == index * group + (lanes >> 8))
        target = jnp.dot(back_rows[...], spread, preferred_element_type=F32)
        for inner in range(group):
            chunk = index * group + inner
            table = one_hot(target[:, inner * 2 * SPAN : (inner + 1) * 2 * SPAN] == columns)
            rows = jnp.concatenate(
                [
                    mixed[which, pl.ds(pl.multiple_of(firsts[chunk, which], 16), SPAN), :]
                    for which in range(2)
                ],
                axis=0,
            )
            result[chunk * CHUNK_ROWS : (chunk + 1) * CHUNK_ROWS, :] = jnp.dot(
                table, rows, preferred_element_type=F32
            ).astype(BF16)
        span = pl.ds(index * group * CHUNK_ROWS, group * CHUNK_ROWS)
        sent.append(pltpu.make_async_copy(result.at[span], out_hbm.at[span], leaving.at[index]))
        sent[index].start()
    for copy in sent:
        copy.wait()


def cluster_call(pool):
    return pl.pallas_call(
        cluster_kernel,
        in_specs=[pl.BlockSpec(memory_space=pl.ANY)],
        out_specs=pl.BlockSpec(memory_space=pl.ANY),
        out_shape=jax.ShapeDtypeStruct((SHARDS * POOL, HD), BF16),
        scratch_shapes=[
            pltpu.VMEM((SHARDS, PACK, HD), BF16),
            pltpu.VMEM((SHARDS, 16, HD), BF16),
            pltpu.VMEM((3, 2, CSIZE + SPAN, HD), BF16),
            pltpu.VMEM((2, CSIZE + SPAN, HD), BF16),
            pltpu.VMEM((2, CSIZE, QBLOCK), F32),
            pltpu.VMEM((2, 1, QBLOCK), F32),
            pltpu.VMEM((2, HD, CSIZE), BF16),
            pltpu.VMEM((CHUNKS, SHARDS), jnp.int32),
            pltpu.VMEM((CHUNKS, SHARDS), jnp.int32),
            pltpu.VMEM((CHUNK_ROWS, CHUNKS), BF16),
            pltpu.VMEM((CHUNKS, SHARDS), jnp.int32),
            pltpu.SMEM((CHUNKS, SHARDS), jnp.int32),
            pltpu.SemaphoreType.DMA((PARTS + 1,)),
            pltpu.SemaphoreType.DMA,
            pltpu.VMEM((SHARDS * POOL, HD), BF16),
            pltpu.SemaphoreType.DMA((PARTS,)),
        ],
        compiler_params=pltpu.CompilerParams(vmem_limit_bytes=VMEM),
        name="cluster",
    )(pool)


def post_kernel(
    back_hbm, slot_hbm, base_hbm, w_hbm, out_hbm, back, slots, base, weights, mix, out, sems, leaving
):
    slot_copy = pltpu.make_async_copy(slot_hbm, slots, sems.at[HC // 2 + 2])
    slot_copy.start()
    copies = []
    for index in range(HC // 2):
        span = pl.ds(index * 2 * REGION, 2 * REGION)
        copies.append(pltpu.make_async_copy(back_hbm.at[span], back.at[span], sems.at[index]))
    copies.append(
        pltpu.make_async_copy(w_hbm.at[pl.ds(HL * HD, HC * HD)], weights, sems.at[HC // 2])
    )
    copies.append(pltpu.make_async_copy(base_hbm, base, sems.at[HC // 2 + 1]))
    for copy in copies:
        copy.start()
    columns = iota((TOK, REGION), 1)
    slot_copy.wait()
    for head in range(HC):
        if head % 2 == 0:
            copies[head // 2].wait()
        table = one_hot(columns == slots[:, head : head + 1])
        mix[:, head * HD : (head + 1) * HD] = jnp.dot(
            table, back[head * REGION : (head + 1) * REGION, :], preferred_element_type=F32
        ).astype(BF16)
    copies[-2].wait()
    copies[-1].wait()
    sent = []
    for index in range(PARTS):
        rows = slice(index * TOK // PARTS, (index + 1) * TOK // PARTS)
        out[rows, :] = (
            base[rows, :] + jnp.dot(mix[rows, :], weights[...], preferred_element_type=F32)
        ).astype(BF16)
        span = pl.ds(index * TOK // PARTS, TOK // PARTS)
        sent.append(pltpu.make_async_copy(out.at[span], out_hbm.at[span], leaving.at[index]))
        sent[index].start()
    for copy in sent:
        copy.wait()


def post_call(back, slot, base, w_output):
    return pl.pallas_call(
        post_kernel,
        in_specs=[
            pl.BlockSpec(memory_space=pl.ANY),
            pl.BlockSpec(memory_space=pl.ANY),
            pl.BlockSpec(memory_space=pl.ANY),
            pl.BlockSpec(memory_space=pl.ANY),
        ],
        out_specs=pl.BlockSpec(memory_space=pl.ANY),
        out_shape=jax.ShapeDtypeStruct((TOK, D), BF16),
        scratch_shapes=[
            pltpu.VMEM((HC * REGION, HD), BF16),
            pltpu.VMEM((TOK, HC), jnp.int32),
            pltpu.VMEM((TOK, D), F32),
            pltpu.VMEM((HC * HD, D), BF16),
            pltpu.VMEM((TOK, HC * HD), BF16),
            pltpu.VMEM((TOK, D), BF16),
            pltpu.SemaphoreType.DMA((HC // 2 + 3,)),
            pltpu.SemaphoreType.DMA((PARTS,)),
        ],
        compiler_params=pltpu.CompilerParams(vmem_limit_bytes=VMEM),
        name="collect",
    )(back, slot, base, w_output)


def token_slots(assignment):
    member = assignment[:, :, None] == jnp.arange(CLUSTERS, dtype=jnp.int32)
    rows = jnp.arange(TOK, dtype=jnp.int32)
    earlier = (rows[:, None] > rows[None, :]).astype(BF16)
    running = jnp.dot(
        earlier, member.astype(BF16).reshape(TOK, HC * CLUSTERS), preferred_element_type=F32
    ).reshape(TOK, HC, CLUSTERS)
    position = jnp.sum(jnp.where(member, running, 0.0), axis=2).astype(jnp.int32)
    return (assignment >> 1) * POOL + slot_of(assignment, position)


def body(activations, norm_gain, w_local, w_cluster, w_output, assignment):
    device = lax.axis_index(AXES)
    placed = pre_call(activations, norm_gain, w_cluster, assignment)
    got_pool = lax.all_to_all(placed, AXES, split_axis=0, concat_axis=0, tiled=True)

    local_qkv = jnp.dot(
        rms_norm(activations, norm_gain), w_local, preferred_element_type=F32
    ).astype(BF16)
    slot = token_slots(assignment)

    local_kv = local_qkv[:, HL * HD :]
    rim = lax.ppermute(local_kv, AXES, [(i, i + 1) for i in range(SHARDS - 1)])
    finished = cluster_call(got_pool)
    finished, rim = lax.optimization_barrier((finished, rim))
    came_back = lax.all_to_all(
        finished.reshape(SHARDS, POOL, HD), AXES, split_axis=0, concat_axis=0, tiled=True
    )
    base = window_call(
        jnp.minimum(device, 1).astype(jnp.int32).reshape(1), local_qkv, rim, activations, w_output
    )
    return post_call(came_back.reshape(SHARDS * POOL, HD), slot, base, w_output)


def solution(mesh):
    in_specs = (P(AXES, None), P(), P(), P(), P(), P(AXES, None))
    out_specs = P(AXES, None)
    return jax.shard_map(body, mesh=mesh, in_specs=in_specs, out_specs=out_specs, check_vma=False)
```

```python
import functools
import math

import jax
import jax.numpy as jnp
from jax import lax
from jax.experimental import pallas as pl
from jax.experimental.pallas import tpu as pltpu
from jax.sharding import PartitionSpec as P

HL = 4
HC = 8
HD = 128
WIN = 512
CSIZE = 2048
CLUSTERS = 32
TOK = 512
D = 1024
SHARDS = 128
POOL = 40
PER_CLUSTER = 28
GROUPS = CLUSTERS // 2
REGION = GROUPS * POOL
MAIN = 32
TAIL = POOL - MAIN
PACK = 3 * MAIN + 4 * TAIL
HEADS_STEP = 2
CHUNK = 4
CHUNKS = SHARDS // CHUNK
CHUNK_ROWS = CHUNK * POOL
SPAN = CHUNK * PER_CLUSTER + 16
QBLOCK = 1024
PARTS = 4
EPSILON = 1e-06
AXES = ("sx", "sy")
VMEM = 60 * 2**20
EXP2_SCALE = HD ** (-0.5) * math.log2(math.e)
NT = (((1,), (1,)), ((), ()))
TN = (((0,), (0,)), ((), ()))
F32 = jnp.float32
BF16 = jnp.bfloat16


def iota(shape, dim):
    return lax.broadcasted_iota(jnp.int32, shape, dim)


def one_hot(condition):
    return jnp.where(condition, 1.0, 0.0).astype(BF16)


def rms_norm(activations, norm_gain):
    values = activations.astype(F32)
    mean_square = jnp.mean(values * values, axis=-1, keepdims=True)
    return (values * lax.rsqrt(mean_square + EPSILON) * norm_gain).astype(BF16)


def slot_of(cluster, position):
    return jnp.where((cluster & 1) == 1, POOL - 1 - position, position)


def pre_kernel(
    act_hbm, gain_ref, w_hbm, asg_ref, out_hbm, act, weights, normed, rows, sizes, stage, arrived, leaving
):
    steps = HC // HEADS_STEP
    width = HEADS_STEP * 3 * HD
    copies = [
        pltpu.make_async_copy(
            w_hbm.at[:, pl.ds(step * width, width)], weights.at[step], arrived.at[step]
        )
        for step in range(steps)
    ]
    act_copy = pltpu.make_async_copy(act_hbm, act, arrived.at[steps])
    act_copy.start()
    for copy in copies:
        copy.start()

    cluster = asg_ref[...]
    spread = one_hot((iota((HC * CLUSTERS, HC), 0) >> 5) == iota((HC * CLUSTERS, HC), 1))
    value = jnp.dot(spread, cluster.astype(F32).astype(BF16), preferred_element_type=F32)
    member = value == (iota((HC * CLUSTERS, TOK), 0) & (CLUSTERS - 1)).astype(F32)
    before = one_hot(iota((TOK, TOK), 0) < iota((TOK, TOK), 1))
    running = jnp.dot(one_hot(member), before, preferred_element_type=F32)
    gather = one_hot(iota((HC, HC * CLUSTERS), 0) == (iota((HC, HC * CLUSTERS), 1) >> 5))
    position = jnp.dot(
        gather, jnp.where(member, running, 0.0).astype(BF16), preferred_element_type=F32
    ).astype(jnp.int32)
    slot = slot_of(cluster, position)
    group = cluster >> 1
    rows[...] = jnp.where(
        slot < MAIN, group * MAIN + slot, GROUPS * MAIN + group * TAIL + slot - MAIN
    )
    sizes[...] = jnp.dot(
        one_hot(member), jnp.ones((TOK, HD), BF16), preferred_element_type=F32
    ).astype(BF16)
    which = iota((GROUPS * TAIL, CLUSTERS), 0)
    pick = one_hot(
        ((which >> 3) * 2 + (which & 7) == iota((GROUPS * TAIL, CLUSTERS), 1)) & ((which & 7) < 2)
    )
    act_copy.wait()
    normed[...] = rms_norm(act[...], gain_ref[...])

    def project(step):
        copies[step].wait()
        return jnp.dot(normed[...], weights[step], preferred_element_type=F32).astype(BF16)

    sent = []
    qkv = project(0)
    for step in range(steps):
        later = project(step + 1) if step + 1 < steps else None
        for inner in range(HEADS_STEP):
            head = step * HEADS_STEP + inner
            table = one_hot(iota((REGION, TOK), 0) == rows[head : head + 1, :])
            placed = jnp.dot(
                table, qkv[:, inner * 3 * HD : (inner + 1) * 3 * HD], preferred_element_type=F32
            )
            groups = slice(head * GROUPS, (head + 1) * GROUPS)
            tails = []
            for kind in range(3):
                part = placed[:, kind * HD : (kind + 1) * HD]
                stage[groups, kind * MAIN : (kind + 1) * MAIN, :] = (
                    part[: GROUPS * MAIN].astype(BF16).reshape(GROUPS, MAIN, HD)
                )
                tails.append(part[GROUPS * MAIN :].reshape(GROUPS, TAIL, HD))
            size = sizes[head * CLUSTERS : (head + 1) * CLUSTERS, :]
            tails.append(
                jnp.dot(pick, size, preferred_element_type=F32).reshape(GROUPS, TAIL, HD)
            )
            stage[groups, 3 * MAIN :, :] = jnp.concatenate(tails, axis=1).astype(BF16)
            span = pl.ds(head * GROUPS, GROUPS)
            sent.append(pltpu.make_async_copy(stage.at[span], out_hbm.at[span], leaving.at[head]))
            sent[head].start()
        qkv = later
    for copy in sent:
        copy.wait()


def pre_call(activations, norm_gain, w_cluster, assignment):
    steps = HC // HEADS_STEP
    return pl.pallas_call(
        pre_kernel,
        in_specs=[
            pl.BlockSpec(memory_space=pl.ANY),
            pl.BlockSpec(memory_space=pltpu.VMEM),
            pl.BlockSpec(memory_space=pl.ANY),
            pl.BlockSpec(memory_space=pltpu.VMEM),
        ],
        out_specs=pl.BlockSpec(memory_space=pl.ANY),
        out_shape=jax.ShapeDtypeStruct((SHARDS, PACK, HD), BF16),
        scratch_shapes=[
            pltpu.VMEM((TOK, D), BF16),
            pltpu.VMEM((steps, D, HEADS_STEP * 3 * HD), BF16),
            pltpu.VMEM((TOK, D), BF16),
            pltpu.VMEM((HC, TOK), jnp.int32),
            pltpu.VMEM((HC * CLUSTERS, HD), BF16),
            pltpu.VMEM((SHARDS, PACK, HD), BF16),
            pltpu.SemaphoreType.DMA((steps + 1,)),
            pltpu.SemaphoreType.DMA((HC,)),
        ],
        compiler_params=pltpu.CompilerParams(vmem_limit_bytes=VMEM),
        name="place",
    )(activations, norm_gain.reshape(1, D), w_cluster, assignment.T)


def softmax_rows(scores):
    highest = jnp.max(scores, axis=-1, keepdims=True)
    raised = jnp.exp2((scores - highest) * EXP2_SCALE)
    total = jnp.sum(raised, axis=-1, keepdims=True)
    return (raised * (1.0 / total)).astype(BF16)


def window_kernel(first_ref, qkv_ref, rim_ref, act_ref, w_ref, out_ref, mix):
    width = HL * HD
    step = 128
    shift = jnp.where(first_ref[0] == 0, WIN, 0)
    for head in range(HL):
        lanes = slice(head * HD, (head + 1) * HD)
        key_lanes = slice(width + head * HD, width + (head + 1) * HD)
        value_lanes = slice(2 * width + head * HD, 2 * width + (head + 1) * HD)
        for low in range(0, TOK, step):
            high = low + step
            query = qkv_ref[low:high, lanes]
            keys = jnp.concatenate([rim_ref[low:, lanes], qkv_ref[:high, key_lanes]], axis=0)
            values = jnp.concatenate(
                [rim_ref[low:, key_lanes], qkv_ref[:high, value_lanes]], axis=0
            )
            scores = lax.dot_general(query, keys, NT, preferred_element_type=F32)
            rows = iota(scores.shape, 0)
            cols = iota(scores.shape, 1)
            allowed = (cols > rows) & (cols <= rows + WIN) & (cols + low >= shift)
            weights = softmax_rows(jnp.where(allowed, scores, -1e30))
            mix[low:high, lanes] = jnp.dot(weights, values, preferred_element_type=F32).astype(BF16)
    out_ref[...] = act_ref[...].astype(F32) + jnp.dot(
        mix[...], w_ref[...], preferred_element_type=F32
    )


def window_call(first, local_qkv, rim, activations, w_output):
    width = HL * HD
    return pl.pallas_call(
        window_kernel,
        grid=(1,),
        in_specs=[
            pl.BlockSpec(memory_space=pltpu.SMEM),
            pl.BlockSpec((TOK, 3 * width), lambda i: (0, 0)),
            pl.BlockSpec((WIN, 2 * width), lambda i: (0, 0)),
            pl.BlockSpec((TOK, D), lambda i: (0, 0)),
            pl.BlockSpec((width, D), lambda i: (0, 0)),
        ],
        out_specs=pl.BlockSpec((TOK, D), lambda i: (0, 0)),
        out_shape=jax.ShapeDtypeStruct((TOK, D), F32),
        scratch_shapes=[pltpu.VMEM((TOK, width), BF16)],
        compiler_params=pltpu.CompilerParams(vmem_limit_bytes=VMEM),
        cost_estimate=pl.CostEstimate(flops=10**10, bytes_accessed=10**7, transcendentals=0),
        name="window",
    )(first, local_qkv, rim, activations, w_output)


def plan_moves(meta, main_rows, tail_rows, back_rows, first_rows):
    source = iota((SHARDS, SHARDS), 0)
    other = iota((SHARDS, SHARDS), 1)
    earlier = one_hot(other < source)
    chunk_earlier = one_hot(other < (source & ~(CHUNK - 1)))
    own_lanes = [(source & (CHUNK - 1)) == (other >> shift) for shift in (5, 3)]
    chunk_of = one_hot(iota((CHUNKS, SHARDS), 0) == (iota((CHUNKS, SHARDS), 1) >> 2))
    leader = one_hot(iota((CHUNKS, SHARDS), 0) * CHUNK == iota((CHUNKS, SHARDS), 1))
    lane = iota((CHUNKS, SHARDS), 1)
    tail_block = meta[...].reshape(SHARDS * 16, HD)
    picked = iota((SHARDS, SHARDS * 16), 1) - iota((SHARDS, SHARDS * 16), 0) * 16

    def by_chunk(values, own):
        return jnp.dot(
            chunk_of, jnp.where(own, values, 0.0).astype(BF16), preferred_element_type=F32
        ).astype(jnp.int32)

    starts, sizes, firsts = [], [], []
    for which in range(2):
        size = jnp.dot(
            one_hot(picked == 8 + which), tail_block, preferred_element_type=F32
        ).astype(BF16)
        start = jnp.dot(earlier, size, preferred_element_type=F32).astype(jnp.int32)
        first = jnp.dot(chunk_earlier, size, preferred_element_type=F32).astype(jnp.int32) >> 4
        local = (start - (first << 4)).astype(F32)
        starts.append([by_chunk(local, own) for own in own_lanes])
        sizes.append([by_chunk(size.astype(F32), own) for own in own_lanes])
        firsts.append(
            jnp.dot(leader, first.astype(F32).astype(BF16), preferred_element_type=F32).astype(
                jnp.int32
            )
            << 4
        )

    def moves(slot, table):
        last = POOL - 1 - slot
        return jnp.where(
            slot < sizes[0][table],
            starts[0][table] + slot,
            jnp.where(last < sizes[1][table], SPAN + starts[1][table] + last, -1),
        )

    main = moves(lane & (MAIN - 1), 0)
    tail = moves(MAIN + (lane & (TAIL - 1)), 1)
    main_rows[...] = main
    tail_rows[...] = tail
    back_rows[...] = (
        jnp.concatenate(
            [
                main.astype(F32).T.reshape(CHUNK, MAIN, CHUNKS),
                tail.astype(F32).T[: CHUNK * TAIL].reshape(CHUNK, TAIL, CHUNKS),
            ],
            axis=1,
        )
        .reshape(CHUNK_ROWS, CHUNKS)
        .astype(BF16)
    )
    first_rows[...] = jnp.where(iota((CHUNKS, SHARDS), 1) == 0, firsts[0], firsts[1])


def cluster_kernel(
    pool_hbm,
    out_hbm,
    pool,
    meta,
    packed,
    mixed,
    scores,
    tops,
    turned,
    main_rows,
    tail_rows,
    back_rows,
    first_rows,
    firsts,
    arrived,
    planned,
    result,
    leaving,
):
    part = SHARDS // PARTS
    head_copy = pltpu.make_async_copy(pool_hbm.at[:, PACK - 16 :, :], meta, arrived.at[PARTS])
    head_copy.start()
    copies = []
    for index in range(PARTS):
        span = pl.ds(index * part, part)
        copies.append(pltpu.make_async_copy(pool_hbm.at[span], pool.at[span], arrived.at[index]))
        copies[index].start()
    packed[:, :, :16] = jnp.zeros((3, 2, 16, HD), BF16)
    mixed[:, CSIZE:] = jnp.zeros((2, SPAN, HD), BF16)
    head_copy.wait()
    plan_moves(meta, main_rows, tail_rows, back_rows, first_rows)
    plan_copy = pltpu.make_async_copy(first_rows, firsts, planned)
    plan_copy.start()
    plan_copy.wait()
    row_ids = iota((2 * SPAN, SHARDS), 0)

    def compact(chunk):
        here = pl.ds(chunk, 1)
        sources = pl.ds(chunk * CHUNK, CHUNK)
        table = jnp.concatenate(
            [
                one_hot(row_ids == main_rows[here, :]),
                one_hot(row_ids == tail_rows[here, :])[:, : CHUNK * TAIL],
            ],
            axis=1,
        )
        tail = pool[sources, 3 * MAIN :, :].astype(F32)
        kinds = []
        for kind in range(3):
            rows = pool[sources, kind * MAIN : (kind + 1) * MAIN, :].reshape(CHUNK * MAIN, HD)
            more = tail[:, kind * TAIL : (kind + 1) * TAIL].reshape(CHUNK * TAIL, HD)
            kinds.append(jnp.concatenate([rows, more.astype(BF16)], axis=0))
        moved = jnp.dot(
            table, jnp.concatenate(kinds, axis=1), preferred_element_type=F32
        ).astype(BF16)
        for which in range(2):
            first = pl.multiple_of(firsts[chunk, which], 16)
            rest = pl.ds(pl.multiple_of(first + 16, 16), SPAN - 16)
            for kind in range(3):
                rows = moved[which * SPAN : (which + 1) * SPAN, kind * HD : (kind + 1) * HD]
                packed[kind, which, pl.ds(first, 16), :] += rows[:16]
                packed[kind, which, rest, :] = rows[16:]

    for index in range(PARTS):
        copies[index].wait()
        pl.loop(index * CHUNKS // PARTS, (index + 1) * CHUNKS // PARTS, unroll=8)(compact)

    for which in range(2):
        for low in range(0, CSIZE, 256):
            turned[which, :, low : low + 256] = packed[2, which, low : low + 256, :].T

    blocks = CSIZE // QBLOCK

    def score(buffer, index):
        which = index // blocks
        place = pl.ds(pl.multiple_of(index % blocks * QBLOCK, QBLOCK), QBLOCK)
        values = lax.dot_general(
            packed[1, which, :CSIZE, :],
            packed[0, which, place, :],
            NT,
            preferred_element_type=F32,
        )
        scores[buffer] = values
        tops[buffer] = jnp.max(values, axis=0, keepdims=True)

    score(0, 0)

    @pl.loop(0, 2 * blocks, step=2)
    def _(pair):
        for inner in range(2):
            index = pair + inner
            which = index // blocks
            place = pl.ds(pl.multiple_of(index % blocks * QBLOCK, QBLOCK), QBLOCK)
            score(1 - inner, jnp.minimum(index + 1, 2 * blocks - 1))
            raised = jnp.exp2((scores[inner] - tops[inner]) * EXP2_SCALE)
            scale = 1.0 / jnp.sum(raised, axis=0, keepdims=True)
            weights = (raised * scale).astype(BF16)
            mix = jnp.dot(turned[which], weights, preferred_element_type=F32)
            mixed[which, place, :] = mix.T.astype(BF16)

    columns = iota((CHUNK_ROWS, 2 * SPAN), 1).astype(F32)
    group = CHUNKS // PARTS
    sent = []
    for index in range(PARTS):
        lanes = iota((CHUNKS, group * 2 * SPAN), 1)
        spread = one_hot(iota((CHUNKS, group * 2 * SPAN), 0) == index * group + (lanes >> 8))
        target = jnp.dot(back_rows[...], spread, preferred_element_type=F32)
        for inner in range(group):
            chunk = index * group + inner
            table = one_hot(target[:, inner * 2 * SPAN : (inner + 1) * 2 * SPAN] == columns)
            rows = jnp.concatenate(
                [
                    mixed[which, pl.ds(pl.multiple_of(firsts[chunk, which], 16), SPAN), :]
                    for which in range(2)
                ],
                axis=0,
            )
            result[chunk * CHUNK_ROWS : (chunk + 1) * CHUNK_ROWS, :] = jnp.dot(
                table, rows, preferred_element_type=F32
            ).astype(BF16)
        span = pl.ds(index * group * CHUNK_ROWS, group * CHUNK_ROWS)
        sent.append(pltpu.make_async_copy(result.at[span], out_hbm.at[span], leaving.at[index]))
        sent[index].start()
    for copy in sent:
        copy.wait()


def cluster_call(pool):
    return pl.pallas_call(
        cluster_kernel,
        in_specs=[pl.BlockSpec(memory_space=pl.ANY)],
        out_specs=pl.BlockSpec(memory_space=pl.ANY),
        out_shape=jax.ShapeDtypeStruct((SHARDS * POOL, HD), BF16),
        scratch_shapes=[
            pltpu.VMEM((SHARDS, PACK, HD), BF16),
            pltpu.VMEM((SHARDS, 16, HD), BF16),
            pltpu.VMEM((3, 2, CSIZE + SPAN, HD), BF16),
            pltpu.VMEM((2, CSIZE + SPAN, HD), BF16),
            pltpu.VMEM((2, CSIZE, QBLOCK), F32),
            pltpu.VMEM((2, 1, QBLOCK), F32),
            pltpu.VMEM((2, HD, CSIZE), BF16),
            pltpu.VMEM((CHUNKS, SHARDS), jnp.int32),
            pltpu.VMEM((CHUNKS, SHARDS), jnp.int32),
            pltpu.VMEM((CHUNK_ROWS, CHUNKS), BF16),
            pltpu.VMEM((CHUNKS, SHARDS), jnp.int32),
            pltpu.SMEM((CHUNKS, SHARDS), jnp.int32),
            pltpu.SemaphoreType.DMA((PARTS + 1,)),
            pltpu.SemaphoreType.DMA,
            pltpu.VMEM((SHARDS * POOL, HD), BF16),
            pltpu.SemaphoreType.DMA((PARTS,)),
        ],
        compiler_params=pltpu.CompilerParams(vmem_limit_bytes=VMEM),
        name="cluster",
    )(pool)


def post_kernel(
    back_hbm, slot_hbm, base_hbm, w_hbm, out_hbm, back, slots, base, weights, mix, out, sems, leaving
):
    slot_copy = pltpu.make_async_copy(slot_hbm, slots, sems.at[HC // 2 + 2])
    slot_copy.start()
    copies = []
    for index in range(HC // 2):
        span = pl.ds(index * 2 * REGION, 2 * REGION)
        copies.append(pltpu.make_async_copy(back_hbm.at[span], back.at[span], sems.at[index]))
    copies.append(
        pltpu.make_async_copy(w_hbm.at[pl.ds(HL * HD, HC * HD)], weights, sems.at[HC // 2])
    )
    copies.append(pltpu.make_async_copy(base_hbm, base, sems.at[HC // 2 + 1]))
    for copy in copies:
        copy.start()
    columns = iota((TOK, REGION), 1)
    slot_copy.wait()
    for head in range(HC):
        if head % 2 == 0:
            copies[head // 2].wait()
        table = one_hot(columns == slots[:, head : head + 1])
        mix[:, head * HD : (head + 1) * HD] = jnp.dot(
            table, back[head * REGION : (head + 1) * REGION, :], preferred_element_type=F32
        ).astype(BF16)
    copies[-2].wait()
    copies[-1].wait()
    sent = []
    for index in range(PARTS):
        rows = slice(index * TOK // PARTS, (index + 1) * TOK // PARTS)
        out[rows, :] = (
            base[rows, :] + jnp.dot(mix[rows, :], weights[...], preferred_element_type=F32)
        ).astype(BF16)
        span = pl.ds(index * TOK // PARTS, TOK // PARTS)
        sent.append(pltpu.make_async_copy(out.at[span], out_hbm.at[span], leaving.at[index]))
        sent[index].start()
    for copy in sent:
        copy.wait()


def post_call(back, slot, base, w_output):
    return pl.pallas_call(
        post_kernel,
        in_specs=[
            pl.BlockSpec(memory_space=pl.ANY),
            pl.BlockSpec(memory_space=pl.ANY),
            pl.BlockSpec(memory_space=pl.ANY),
            pl.BlockSpec(memory_space=pl.ANY),
        ],
        out_specs=pl.BlockSpec(memory_space=pl.ANY),
        out_shape=jax.ShapeDtypeStruct((TOK, D), BF16),
        scratch_shapes=[
            pltpu.VMEM((HC * REGION, HD), BF16),
            pltpu.VMEM((TOK, HC), jnp.int32),
            pltpu.VMEM((TOK, D), F32),
            pltpu.VMEM((HC * HD, D), BF16),
            pltpu.VMEM((TOK, HC * HD), BF16),
            pltpu.VMEM((TOK, D), BF16),
            pltpu.SemaphoreType.DMA((HC // 2 + 3,)),
            pltpu.SemaphoreType.DMA((PARTS,)),
        ],
        compiler_params=pltpu.CompilerParams(vmem_limit_bytes=VMEM),
        name="collect",
    )(back, slot, base, w_output)


def token_slots(assignment):
    member = assignment[:, :, None] == jnp.arange(CLUSTERS, dtype=jnp.int32)
    rows = jnp.arange(TOK, dtype=jnp.int32)
    earlier = (rows[:, None] > rows[None, :]).astype(BF16)
    running = jnp.dot(
        earlier, member.astype(BF16).reshape(TOK, HC * CLUSTERS), preferred_element_type=F32
    ).reshape(TOK, HC, CLUSTERS)
    position = jnp.sum(jnp.where(member, running, 0.0), axis=2).astype(jnp.int32)
    return (assignment >> 1) * POOL + slot_of(assignment, position)


def body(activations, norm_gain, w_local, w_cluster, w_output, assignment):
    device = lax.axis_index(AXES)
    placed = pre_call(activations, norm_gain, w_cluster, assignment)
    got_pool = lax.all_to_all(placed, AXES, split_axis=0, concat_axis=0, tiled=True)

    local_qkv = jnp.dot(
        rms_norm(activations, norm_gain), w_local, preferred_element_type=F32
    ).astype(BF16)
    slot = token_slots(assignment)

    local_kv = local_qkv[:, HL * HD :]
    rim = lax.ppermute(local_kv, AXES, [(i, i + 1) for i in range(SHARDS - 1)])
    finished = cluster_call(got_pool)
    finished, rim = lax.optimization_barrier((finished, rim))
    came_back = lax.all_to_all(
        finished.reshape(SHARDS, POOL, HD), AXES, split_axis=0, concat_axis=0, tiled=True
    )
    base = window_call(
        jnp.minimum(device, 1).astype(jnp.int32).reshape(1), local_qkv, rim, activations, w_output
    )
    return post_call(came_back.reshape(SHARDS * POOL, HD), slot, base, w_output)


def solution(mesh):
    in_specs = (P(AXES, None), P(), P(), P(), P(), P(AXES, None))
    out_specs = P(AXES, None)
    return jax.shard_map(body, mesh=mesh, in_specs=in_specs, out_specs=out_specs, check_vma=False)
```

```python
import functools
import math

import jax
import jax.numpy as jnp
from jax import lax
from jax.experimental import pallas as pl
from jax.experimental.pallas import tpu as pltpu
from jax.sharding import PartitionSpec as P

HL = 4
HC = 8
HD = 128
WIN = 512
CSIZE = 2048
CLUSTERS = 32
TOK = 512
D = 1024
SHARDS = 128
POOL = 40
PER_CLUSTER = 28
GROUPS = CLUSTERS // 2
REGION = GROUPS * POOL
MAIN = 32
TAIL = POOL - MAIN
PACK = 3 * MAIN + 4 * TAIL
HEADS_STEP = 4
CHUNK = 4
CHUNKS = SHARDS // CHUNK
CHUNK_ROWS = CHUNK * POOL
SPAN = CHUNK * PER_CLUSTER + 16
QBLOCK = 1024
PARTS = 4
EPSILON = 1e-06
AXES = ("sx", "sy")
VMEM = 60 * 2**20
EXP2_SCALE = HD ** (-0.5) * math.log2(math.e)
NT = (((1,), (1,)), ((), ()))
TN = (((0,), (0,)), ((), ()))
F32 = jnp.float32
BF16 = jnp.bfloat16


def iota(shape, dim):
    return lax.broadcasted_iota(jnp.int32, shape, dim)


def one_hot(condition):
    return jnp.where(condition, 1.0, 0.0).astype(BF16)


def rms_norm(activations, norm_gain):
    values = activations.astype(F32)
    mean_square = jnp.mean(values * values, axis=-1, keepdims=True)
    return (values * lax.rsqrt(mean_square + EPSILON) * norm_gain).astype(BF16)


def slot_of(cluster, position):
    return jnp.where((cluster & 1) == 1, POOL - 1 - position, position)


def pre_kernel(
    act_hbm, gain_ref, w_hbm, asg_ref, out_hbm, act, weights, normed, rows, sizes, stage, arrived, leaving
):
    steps = HC // HEADS_STEP
    width = HEADS_STEP * 3 * HD
    copies = [
        pltpu.make_async_copy(
            w_hbm.at[:, pl.ds(step * width, width)], weights.at[step], arrived.at[step]
        )
        for step in range(steps)
    ]
    act_copy = pltpu.make_async_copy(act_hbm, act, arrived.at[steps])
    act_copy.start()
    for copy in copies:
        copy.start()

    cluster = asg_ref[...]
    spread = one_hot((iota((HC * CLUSTERS, HC), 0) >> 5) == iota((HC * CLUSTERS, HC), 1))
    value = jnp.dot(spread, cluster.astype(F32).astype(BF16), preferred_element_type=F32)
    member = value == (iota((HC * CLUSTERS, TOK), 0) & (CLUSTERS - 1)).astype(F32)
    before = one_hot(iota((TOK, TOK), 0) < iota((TOK, TOK), 1))
    running = jnp.dot(one_hot(member), before, preferred_element_type=F32)
    gather = one_hot(iota((HC, HC * CLUSTERS), 0) == (iota((HC, HC * CLUSTERS), 1) >> 5))
    position = jnp.dot(
        gather, jnp.where(member, running, 0.0).astype(BF16), preferred_element_type=F32
    ).astype(jnp.int32)
    slot = slot_of(cluster, position)
    group = cluster >> 1
    rows[...] = jnp.where(
        slot < MAIN, group * MAIN + slot, GROUPS * MAIN + group * TAIL + slot - MAIN
    )
    sizes[...] = jnp.dot(
        one_hot(member), jnp.ones((TOK, HD), BF16), preferred_element_type=F32
    ).astype(BF16)
    which = iota((GROUPS * TAIL, CLUSTERS), 0)
    pick = one_hot(
        ((which >> 3) * 2 + (which & 7) == iota((GROUPS * TAIL, CLUSTERS), 1)) & ((which & 7) < 2)
    )
    act_copy.wait()
    normed[...] = rms_norm(act[...], gain_ref[...])

    def project(step):
        copies[step].wait()
        return jnp.dot(normed[...], weights[step], preferred_element_type=F32).astype(BF16)

    sent = []
    qkv = project(0)
    for step in range(steps):
        later = project(step + 1) if step + 1 < steps else None
        for inner in range(HEADS_STEP):
            head = step * HEADS_STEP + inner
            table = one_hot(iota((REGION, TOK), 0) == rows[head : head + 1, :])
            placed = jnp.dot(
                table, qkv[:, inner * 3 * HD : (inner + 1) * 3 * HD], preferred_element_type=F32
            )
            groups = slice(head * GROUPS, (head + 1) * GROUPS)
            tails = []
            for kind in range(3):
                part = placed[:, kind * HD : (kind + 1) * HD]
                stage[groups, kind * MAIN : (kind + 1) * MAIN, :] = (
                    part[: GROUPS * MAIN].astype(BF16).reshape(GROUPS, MAIN, HD)
                )
                tails.append(part[GROUPS * MAIN :].reshape(GROUPS, TAIL, HD))
            size = sizes[head * CLUSTERS : (head + 1) * CLUSTERS, :]
            tails.append(
                jnp.dot(pick, size, preferred_element_type=F32).reshape(GROUPS, TAIL, HD)
            )
            stage[groups, 3 * MAIN :, :] = jnp.concatenate(tails, axis=1).astype(BF16)
        span = pl.ds(step * HEADS_STEP * GROUPS, HEADS_STEP * GROUPS)
        sent.append(pltpu.make_async_copy(stage.at[span], out_hbm.at[span], leaving.at[step]))
        sent[step].start()
        qkv = later
    for copy in sent:
        copy.wait()


def pre_call(activations, norm_gain, w_cluster, assignment):
    steps = HC // HEADS_STEP
    return pl.pallas_call(
        pre_kernel,
        in_specs=[
            pl.BlockSpec(memory_space=pl.ANY),
            pl.BlockSpec(memory_space=pltpu.VMEM),
            pl.BlockSpec(memory_space=pl.ANY),
            pl.BlockSpec(memory_space=pltpu.VMEM),
        ],
        out_specs=pl.BlockSpec(memory_space=pl.ANY),
        out_shape=jax.ShapeDtypeStruct((SHARDS, PACK, HD), BF16),
        scratch_shapes=[
            pltpu.VMEM((TOK, D), BF16),
            pltpu.VMEM((steps, D, HEADS_STEP * 3 * HD), BF16),
            pltpu.VMEM((TOK, D), BF16),
            pltpu.VMEM((HC, TOK), jnp.int32),
            pltpu.VMEM((HC * CLUSTERS, HD), BF16),
            pltpu.VMEM((SHARDS, PACK, HD), BF16),
            pltpu.SemaphoreType.DMA((steps + 1,)),
            pltpu.SemaphoreType.DMA((steps,)),
        ],
        compiler_params=pltpu.CompilerParams(vmem_limit_bytes=VMEM),
        name="place",
    )(activations, norm_gain.reshape(1, D), w_cluster, assignment.T)


def softmax_rows(scores):
    highest = jnp.max(scores, axis=-1, keepdims=True)
    raised = jnp.exp2((scores - highest) * EXP2_SCALE)
    total = jnp.sum(raised, axis=-1, keepdims=True)
    return (raised * (1.0 / total)).astype(BF16)


def window_kernel(first_ref, qkv_ref, rim_ref, act_ref, w_ref, out_ref, mix):
    width = HL * HD
    step = 128
    shift = jnp.where(first_ref[0] == 0, WIN, 0)
    for head in range(HL):
        lanes = slice(head * HD, (head + 1) * HD)
        key_lanes = slice(width + head * HD, width + (head + 1) * HD)
        value_lanes = slice(2 * width + head * HD, 2 * width + (head + 1) * HD)
        for low in range(0, TOK, step):
            high = low + step
            query = qkv_ref[low:high, lanes]
            keys = jnp.concatenate([rim_ref[low:, lanes], qkv_ref[:high, key_lanes]], axis=0)
            values = jnp.concatenate(
                [rim_ref[low:, key_lanes], qkv_ref[:high, value_lanes]], axis=0
            )
            scores = lax.dot_general(query, keys, NT, preferred_element_type=F32)
            rows = iota(scores.shape, 0)
            cols = iota(scores.shape, 1)
            allowed = (cols > rows) & (cols <= rows + WIN) & (cols + low >= shift)
            weights = softmax_rows(jnp.where(allowed, scores, -1e30))
            mix[low:high, lanes] = jnp.dot(weights, values, preferred_element_type=F32).astype(BF16)
    out_ref[...] = act_ref[...].astype(F32) + jnp.dot(
        mix[...], w_ref[...], preferred_element_type=F32
    )


def window_call(first, local_qkv, rim, activations, w_output):
    width = HL * HD
    return pl.pallas_call(
        window_kernel,
        grid=(1,),
        in_specs=[
            pl.BlockSpec(memory_space=pltpu.SMEM),
            pl.BlockSpec((TOK, 3 * width), lambda i: (0, 0)),
            pl.BlockSpec((WIN, 2 * width), lambda i: (0, 0)),
            pl.BlockSpec((TOK, D), lambda i: (0, 0)),
            pl.BlockSpec((width, D), lambda i: (0, 0)),
        ],
        out_specs=pl.BlockSpec((TOK, D), lambda i: (0, 0)),
        out_shape=jax.ShapeDtypeStruct((TOK, D), F32),
        scratch_shapes=[pltpu.VMEM((TOK, width), BF16)],
        compiler_params=pltpu.CompilerParams(vmem_limit_bytes=VMEM),
        cost_estimate=pl.CostEstimate(flops=10**10, bytes_accessed=10**7, transcendentals=0),
        name="window",
    )(first, local_qkv, rim, activations, w_output)


def plan_moves(meta, main_rows, tail_rows, back_rows, first_rows):
    source = iota((SHARDS, SHARDS), 0)
    other = iota((SHARDS, SHARDS), 1)
    earlier = one_hot(other < source)
    chunk_earlier = one_hot(other < (source & ~(CHUNK - 1)))
    own_lanes = [(source & (CHUNK - 1)) == (other >> shift) for shift in (5, 3)]
    chunk_of = one_hot(iota((CHUNKS, SHARDS), 0) == (iota((CHUNKS, SHARDS), 1) >> 2))
    leader = one_hot(iota((CHUNKS, SHARDS), 0) * CHUNK == iota((CHUNKS, SHARDS), 1))
    lane = iota((CHUNKS, SHARDS), 1)
    tail_block = meta[...].reshape(SHARDS * 16, HD)
    picked = iota((SHARDS, SHARDS * 16), 1) - iota((SHARDS, SHARDS * 16), 0) * 16

    def by_chunk(values, own):
        return jnp.dot(
            chunk_of, jnp.where(own, values, 0.0).astype(BF16), preferred_element_type=F32
        ).astype(jnp.int32)

    starts, sizes, firsts = [], [], []
    for which in range(2):
        size = jnp.dot(
            one_hot(picked == 8 + which), tail_block, preferred_element_type=F32
        ).astype(BF16)
        start = jnp.dot(earlier, size, preferred_element_type=F32).astype(jnp.int32)
        first = jnp.dot(chunk_earlier, size, preferred_element_type=F32).astype(jnp.int32) >> 4
        local = (start - (first << 4)).astype(F32)
        starts.append([by_chunk(local, own) for own in own_lanes])
        sizes.append([by_chunk(size.astype(F32), own) for own in own_lanes])
        firsts.append(
            jnp.dot(leader, first.astype(F32).astype(BF16), preferred_element_type=F32).astype(
                jnp.int32
            )
            << 4
        )

    def moves(slot, table):
        last = POOL - 1 - slot
        return jnp.where(
            slot < sizes[0][table],
            starts[0][table] + slot,
            jnp.where(last < sizes[1][table], SPAN + starts[1][table] + last, -1),
        )

    main = moves(lane & (MAIN - 1), 0)
    tail = moves(MAIN + (lane & (TAIL - 1)), 1)
    main_rows[...] = main
    tail_rows[...] = tail
    back_rows[...] = (
        jnp.concatenate(
            [
                main.astype(F32).T.reshape(CHUNK, MAIN, CHUNKS),
                tail.astype(F32).T[: CHUNK * TAIL].reshape(CHUNK, TAIL, CHUNKS),
            ],
            axis=1,
        )
        .reshape(CHUNK_ROWS, CHUNKS)
        .astype(BF16)
    )
    first_rows[...] = jnp.where(iota((CHUNKS, SHARDS), 1) == 0, firsts[0], firsts[1])


def cluster_kernel(
    pool_hbm,
    out_hbm,
    pool,
    meta,
    packed,
    mixed,
    scores,
    tops,
    turned,
    main_rows,
    tail_rows,
    back_rows,
    first_rows,
    firsts,
    arrived,
    planned,
    result,
    leaving,
):
    part = SHARDS // PARTS
    head_copy = pltpu.make_async_copy(pool_hbm.at[:, PACK - 16 :, :], meta, arrived.at[PARTS])
    head_copy.start()
    copies = []
    for index in range(PARTS):
        span = pl.ds(index * part, part)
        copies.append(pltpu.make_async_copy(pool_hbm.at[span], pool.at[span], arrived.at[index]))
        copies[index].start()
    packed[:, :, :16] = jnp.zeros((3, 2, 16, HD), BF16)
    mixed[:, CSIZE:] = jnp.zeros((2, SPAN, HD), BF16)
    head_copy.wait()
    plan_moves(meta, main_rows, tail_rows, back_rows, first_rows)
    plan_copy = pltpu.make_async_copy(first_rows, firsts, planned)
    plan_copy.start()
    plan_copy.wait()
    row_ids = iota((2 * SPAN, SHARDS), 0)

    def compact(chunk):
        here = pl.ds(chunk, 1)
        sources = pl.ds(chunk * CHUNK, CHUNK)
        table = jnp.concatenate(
            [
                one_hot(row_ids == main_rows[here, :]),
                one_hot(row_ids == tail_rows[here, :])[:, : CHUNK * TAIL],
            ],
            axis=1,
        )
        tail = pool[sources, 3 * MAIN :, :].astype(F32)
        kinds = []
        for kind in range(3):
            rows = pool[sources, kind * MAIN : (kind + 1) * MAIN, :].reshape(CHUNK * MAIN, HD)
            more = tail[:, kind * TAIL : (kind + 1) * TAIL].reshape(CHUNK * TAIL, HD)
            kinds.append(jnp.concatenate([rows, more.astype(BF16)], axis=0))
        moved = jnp.dot(
            table, jnp.concatenate(kinds, axis=1), preferred_element_type=F32
        ).astype(BF16)
        for which in range(2):
            first = pl.multiple_of(firsts[chunk, which], 16)
            rest = pl.ds(pl.multiple_of(first + 16, 16), SPAN - 16)
            for kind in range(3):
                rows = moved[which * SPAN : (which + 1) * SPAN, kind * HD : (kind + 1) * HD]
                packed[kind, which, pl.ds(first, 16), :] += rows[:16]
                packed[kind, which, rest, :] = rows[16:]

    for index in range(PARTS):
        copies[index].wait()
        pl.loop(index * CHUNKS // PARTS, (index + 1) * CHUNKS // PARTS, unroll=8)(compact)

    for which in range(2):
        for low in range(0, CSIZE, 256):
            turned[which, :, low : low + 256] = packed[2, which, low : low + 256, :].T

    blocks = CSIZE // QBLOCK

    def score(buffer, index):
        which = index // blocks
        place = pl.ds(pl.multiple_of(index % blocks * QBLOCK, QBLOCK), QBLOCK)
        values = lax.dot_general(
            packed[1, which, :CSIZE, :],
            packed[0, which, place, :],
            NT,
            preferred_element_type=F32,
        )
        scores[buffer] = values
        tops[buffer] = jnp.max(values, axis=0, keepdims=True)

    score(0, 0)

    @pl.loop(0, 2 * blocks, step=2)
    def _(pair):
        for inner in range(2):
            index = pair + inner
            which = index // blocks
            place = pl.ds(pl.multiple_of(index % blocks * QBLOCK, QBLOCK), QBLOCK)
            score(1 - inner, jnp.minimum(index + 1, 2 * blocks - 1))
            raised = jnp.exp2((scores[inner] - tops[inner]) * EXP2_SCALE)
            scale = 1.0 / jnp.sum(raised, axis=0, keepdims=True)
            weights = (raised * scale).astype(BF16)
            mix = jnp.dot(turned[which], weights, preferred_element_type=F32)
            mixed[which, place, :] = mix.T.astype(BF16)

    columns = iota((CHUNK_ROWS, 2 * SPAN), 1).astype(F32)
    group = CHUNKS // PARTS
    sent = []
    for index in range(PARTS):
        lanes = iota((CHUNKS, group * 2 * SPAN), 1)
        spread = one_hot(iota((CHUNKS, group * 2 * SPAN), 0) == index * group + (lanes >> 8))
        target = jnp.dot(back_rows[...], spread, preferred_element_type=F32)
        for inner in range(group):
            chunk = index * group + inner
            table = one_hot(target[:, inner * 2 * SPAN : (inner + 1) * 2 * SPAN] == columns)
            rows = jnp.concatenate(
                [
                    mixed[which, pl.ds(pl.multiple_of(firsts[chunk, which], 16), SPAN), :]
                    for which in range(2)
                ],
                axis=0,
            )
            result[chunk * CHUNK_ROWS : (chunk + 1) * CHUNK_ROWS, :] = jnp.dot(
                table, rows, preferred_element_type=F32
            ).astype(BF16)
        span = pl.ds(index * group * CHUNK_ROWS, group * CHUNK_ROWS)
        sent.append(pltpu.make_async_copy(result.at[span], out_hbm.at[span], leaving.at[index]))
        sent[index].start()
    for copy in sent:
        copy.wait()


def cluster_call(pool):
    return pl.pallas_call(
        cluster_kernel,
        in_specs=[pl.BlockSpec(memory_space=pl.ANY)],
        out_specs=pl.BlockSpec(memory_space=pl.ANY),
        out_shape=jax.ShapeDtypeStruct((SHARDS * POOL, HD), BF16),
        scratch_shapes=[
            pltpu.VMEM((SHARDS, PACK, HD), BF16),
            pltpu.VMEM((SHARDS, 16, HD), BF16),
            pltpu.VMEM((3, 2, CSIZE + SPAN, HD), BF16),
            pltpu.VMEM((2, CSIZE + SPAN, HD), BF16),
            pltpu.VMEM((2, CSIZE, QBLOCK), F32),
            pltpu.VMEM((2, 1, QBLOCK), F32),
            pltpu.VMEM((2, HD, CSIZE), BF16),
            pltpu.VMEM((CHUNKS, SHARDS), jnp.int32),
            pltpu.VMEM((CHUNKS, SHARDS), jnp.int32),
            pltpu.VMEM((CHUNK_ROWS, CHUNKS), BF16),
            pltpu.VMEM((CHUNKS, SHARDS), jnp.int32),
            pltpu.SMEM((CHUNKS, SHARDS), jnp.int32),
            pltpu.SemaphoreType.DMA((PARTS + 1,)),
            pltpu.SemaphoreType.DMA,
            pltpu.VMEM((SHARDS * POOL, HD), BF16),
            pltpu.SemaphoreType.DMA((PARTS,)),
        ],
        compiler_params=pltpu.CompilerParams(vmem_limit_bytes=VMEM),
        name="cluster",
    )(pool)


def post_kernel(
    back_hbm, slot_hbm, base_hbm, w_hbm, out_hbm, back, slots, base, weights, mix, out, sems, leaving
):
    slot_copy = pltpu.make_async_copy(slot_hbm, slots, sems.at[HC // 2 + 2])
    slot_copy.start()
    copies = []
    for index in range(HC // 2):
        span = pl.ds(index * 2 * REGION, 2 * REGION)
        copies.append(pltpu.make_async_copy(back_hbm.at[span], back.at[span], sems.at[index]))
    copies.append(
        pltpu.make_async_copy(w_hbm.at[pl.ds(HL * HD, HC * HD)], weights, sems.at[HC // 2])
    )
    copies.append(pltpu.make_async_copy(base_hbm, base, sems.at[HC // 2 + 1]))
    for copy in copies:
        copy.start()
    columns = iota((TOK, REGION), 1)
    slot_copy.wait()
    for head in range(HC):
        if head % 2 == 0:
            copies[head // 2].wait()
        table = one_hot(columns == slots[:, head : head + 1])
        mix[:, head * HD : (head + 1) * HD] = jnp.dot(
            table, back[head * REGION : (head + 1) * REGION, :], preferred_element_type=F32
        ).astype(BF16)
    copies[-2].wait()
    copies[-1].wait()
    sent = []
    for index in range(PARTS):
        rows = slice(index * TOK // PARTS, (index + 1) * TOK // PARTS)
        out[rows, :] = (
            base[rows, :] + jnp.dot(mix[rows, :], weights[...], preferred_element_type=F32)
        ).astype(BF16)
        span = pl.ds(index * TOK // PARTS, TOK // PARTS)
        sent.append(pltpu.make_async_copy(out.at[span], out_hbm.at[span], leaving.at[index]))
        sent[index].start()
    for copy in sent:
        copy.wait()


def post_call(back, slot, base, w_output):
    return pl.pallas_call(
        post_kernel,
        in_specs=[
            pl.BlockSpec(memory_space=pl.ANY),
            pl.BlockSpec(memory_space=pl.ANY),
            pl.BlockSpec(memory_space=pl.ANY),
            pl.BlockSpec(memory_space=pl.ANY),
        ],
        out_specs=pl.BlockSpec(memory_space=pl.ANY),
        out_shape=jax.ShapeDtypeStruct((TOK, D), BF16),
        scratch_shapes=[
            pltpu.VMEM((HC * REGION, HD), BF16),
            pltpu.VMEM((TOK, HC), jnp.int32),
            pltpu.VMEM((TOK, D), F32),
            pltpu.VMEM((HC * HD, D), BF16),
            pltpu.VMEM((TOK, HC * HD), BF16),
            pltpu.VMEM((TOK, D), BF16),
            pltpu.SemaphoreType.DMA((HC // 2 + 3,)),
            pltpu.SemaphoreType.DMA((PARTS,)),
        ],
        compiler_params=pltpu.CompilerParams(vmem_limit_bytes=VMEM),
        name="collect",
    )(back, slot, base, w_output)


def token_slots(assignment):
    member = assignment[:, :, None] == jnp.arange(CLUSTERS, dtype=jnp.int32)
    rows = jnp.arange(TOK, dtype=jnp.int32)
    earlier = (rows[:, None] > rows[None, :]).astype(BF16)
    running = jnp.dot(
        earlier, member.astype(BF16).reshape(TOK, HC * CLUSTERS), preferred_element_type=F32
    ).reshape(TOK, HC, CLUSTERS)
    position = jnp.sum(jnp.where(member, running, 0.0), axis=2).astype(jnp.int32)
    return (assignment >> 1) * POOL + slot_of(assignment, position)


def body(activations, norm_gain, w_local, w_cluster, w_output, assignment):
    device = lax.axis_index(AXES)
    placed = pre_call(activations, norm_gain, w_cluster, assignment)
    got_pool = lax.all_to_all(placed, AXES, split_axis=0, concat_axis=0, tiled=True)

    local_qkv = jnp.dot(
        rms_norm(activations, norm_gain), w_local, preferred_element_type=F32
    ).astype(BF16)
    slot = token_slots(assignment)

    local_kv = local_qkv[:, HL * HD :]
    rim = lax.ppermute(local_kv, AXES, [(i, i + 1) for i in range(SHARDS - 1)])
    finished = cluster_call(got_pool)
    finished, rim = lax.optimization_barrier((finished, rim))
    came_back = lax.all_to_all(
        finished.reshape(SHARDS, POOL, HD), AXES, split_axis=0, concat_axis=0, tiled=True
    )
    base = window_call(
        jnp.minimum(device, 1).astype(jnp.int32).reshape(1), local_qkv, rim, activations, w_output
    )
    return post_call(came_back.reshape(SHARDS * POOL, HD), slot, base, w_output)


def solution(mesh):
    in_specs = (P(AXES, None), P(), P(), P(), P(), P(AXES, None))
    out_specs = P(AXES, None)
    return jax.shard_map(body, mesh=mesh, in_specs=in_specs, out_specs=out_specs, check_vma=False)
```
